512 devices in a mesh: dp: 16 (over z_lo, x), ctx: 32 (over y, z_hi, core).
Axes of the slice: x: 4, y: 8, z: 8 (z_hi: 2, z_lo: 4; z = z_hi * 4 + z_lo), core: 2. Of those that a mesh axis runs over, the one named last changes fastest.
Arguments:
- queries: bfloat16 [8192, 8192], P('ctx', 'dp'), may hold values from -150 to 150
- key_rows: bfloat16 [8192, 8192], P('ctx', 'dp'), may hold values from -10 to 10
- value_rows: bfloat16 [8192, 8192], P('ctx', 'dp'), may hold values from -6 to 6
- lengths: int32 [64], replicated, may hold values from 1 to 2048, 8192 in all
- w_first: bfloat16 [8192, 2048], P('dp'), may hold values from -0.25 to 0.25
- w_noise: bfloat16 [128, 2048], replicated, may hold values from -0.5 to 0.5
- w_out: bfloat16 [2048, 128], replicated, may hold values from -0.125 to 0.125
- noise_draws: bfloat16 [8192, 8, 128], P('ctx'), may hold values from -6 to 6
- target: bfloat16 [8192, 128], P('ctx'), may hold values from -6 to 6
- loss_weights: float32 [8192], P('ctx'), may hold values from 0.25 to 4
Outputs:
- attended: bfloat16 [8192, 8192], P('ctx', 'dp')
- losses: float32 [32, 256], P('ctx', 'dp')
- first_grad: bfloat16 [2048, 8192], P('ctx', 'dp')
The draws below stay inside these ranges and needn't reach their ends.
Inputs may be any that keep to these rules, and one draw needn't show every extreme that they name: `lengths`: lengths fill the 8192 positions in order; the longest document is exactly 2048 positions.
All inputs are finite; a program needn't handle non-finite values.
Results may differ from the reference program's by a relative error of at most 0.02.
Values may be sent and summed in bfloat16 or wider, within the bound.
No kernel may reach another device: no remote copies, remote signals or barrier semaphores. Data moves between devices by JAX's collectives and lax.ppermute only.
A program may use at most 64 MiB of HBM per device.

```python
import math
import jax
import jax.numpy as jnp
import numpy as np
from jax import lax

TOK_DEV = 256
HD = 128
FFH = 2048
LAT = 128
NZ = 128
SAMPLES = 8
HEADS = 64
FEAT = 8192
BLOCKS = 32
TOKENS = 8192
NEAR = 8
DOC_MOST = 2048
DOCS = 64


def shared_rows(key):
    return jnp.clip(jax.random.normal(key, (TOKENS, HEADS * HD), jnp.float32), -6.0, 6.0)


def draw_queries(key, part):
    key = jax.random.fold_in(key, 11)
    own_key = jax.random.fold_in(key, 0)
    own = jnp.clip(jax.random.normal(own_key, (TOKENS, HEADS * HD), jnp.float32), -6.0, 6.0)
    result = own
    return result.astype(jnp.bfloat16)


def draw_key_rows(key, part):
    common = shared_rows(key)
    result = common
    return result.astype(jnp.bfloat16)


def steps_of(key, shape, cuts, smallest, top_value):
    def one(position, shards_of):
        steps = jax.random.uniform(jax.random.fold_in(jax.random.fold_in(key, 6), position), (shards_of,), jnp.float32, smallest / len(cuts), top_value / len(cuts))
        return jnp.repeat(jnp.exp(steps), shape[position] // shards_of).reshape((-1,) + (1,) * (len(shape) - position - 1))

    gain = one(*cuts[0])
    for cut in cuts[1:]:
        gain = gain * one(*cut)
    return gain


def split_up(number_of, total, bound, slope):
    loads = [(1 << 20) // math.isqrt(grade ** slope) + 1 for grade in range(2, number_of + 1)]
    surplus, given = total - bound - (number_of - 1), [1] * (number_of - 1)
    while surplus > 0:
        candidates = [i for i in range(number_of - 1) if given[i] < bound]
        whole, left = sum([loads[i] for i in candidates]), surplus
        for i in candidates:
            more = min(bound - given[i], max(1, left * loads[i] // whole), surplus)
            given[i] = given[i] + more
            surplus = surplus - more
    return np.array([bound] + given)


def ragged(key, amount, total, reach, slope):
    if amount == 2:
        one = jax.random.randint(key, (), max(1, total - reach), min(reach, total - 1) + 1)
        return jnp.stack([one, total - one])
    sizes = jnp.asarray(split_up(amount, total, reach, slope), jnp.int32)
    twos = (amount - 1) // 2
    source_of, receiver = sizes[1:1 + 2 * twos:2], sizes[2:2 + 2 * twos:2]
    slack = jnp.minimum(source_of - 1, reach - receiver)
    passed = jax.random.randint(jax.random.fold_in(key, 1), (twos,), 0, 1 << 20) % (slack + 1)
    sizes = sizes.at[1:1 + 2 * twos:2].set(source_of - passed).at[2:2 + 2 * twos:2].set(receiver + passed)
    return sizes[jax.random.permutation(jax.random.fold_in(key, 2), amount)]


def scatter_about(key, dims, scale, reach, pieces=(), held_as=jnp.bfloat16):
    entries = jax.random.normal(key, dims, jnp.float32) * scale
    if len(pieces) > 0:
        entries = steps_of(key, dims, pieces, -0.22, 0.18) * entries
    return jnp.clip(entries, min=-reach, max=reach).astype(held_as)


def setup_inputs(seed: int = 0) -> dict:
    streams_of = jax.random.split(jax.random.key(seed), 11)
    queries = draw_queries(jax.random.fold_in(streams_of[10], 71), 0)
    key_rows = draw_key_rows(jax.random.fold_in(streams_of[10], 71), 0)
    value_rows = scatter_about(streams_of[2], (TOKENS, FEAT), 1.0, 6.0, ((0, 32), (1, 16)))
    lengths = ragged(streams_of[3], DOCS, TOKENS, DOC_MOST, 2).astype(jnp.int32)
    w_first = scatter_about(streams_of[4], (FEAT, FFH), (FEAT // 16) ** -0.5, 0.25, ((0, 16),))
    w_noise = scatter_about(streams_of[5], (NZ, FFH), NZ ** -0.5, 0.5)
    w_out = scatter_about(streams_of[6], (FFH, LAT), FFH ** -0.5, 0.125)
    noise_draws = scatter_about(streams_of[7], (TOKENS, SAMPLES, NZ), 1.0, 6.0, ((0, 32),))
    target = scatter_about(streams_of[8], (TOKENS, LAT), 1.0, 6.0, ((0, 32),))
    loss_weights = jnp.clip(jnp.exp(math.log(4.0) - 2.7725887 * jax.random.uniform(streams_of[9], (TOKENS,), jnp.float32) ** steps_of(streams_of[9], (TOKENS,), ((0, 32),), -0.2, 0.2)), 0.25, 4.0)
    return dict(queries=queries, key_rows=key_rows, value_rows=value_rows, lengths=lengths, w_first=w_first, w_noise=w_noise, w_out=w_out, noise_draws=noise_draws, target=target, loss_weights=loss_weights)


EPS = 1e-05

def doc_index(lengths, positions):
    ends = jnp.cumsum(lengths)
    return lax.optimization_barrier(jnp.sum((ends[None, :] <= positions[:, None]).astype(jnp.int32), axis=1))

def attend(queries, key_rows, value_rows, query_pos, key_pos, lengths, heads):
    count = queries.shape[0]
    width = queries.shape[1] // heads
    q_heads = queries.reshape(count, heads, width).astype(jnp.float32)
    k_heads = key_rows.reshape(-1, heads, width).astype(jnp.float32)
    v_heads = value_rows.reshape(-1, heads, width).astype(jnp.float32)
    scores = jnp.einsum('qhd,khd->hqk', q_heads, k_heads) * (1.0 / math.sqrt(width))
    allowed = doc_index(lengths, query_pos)[:, None] == doc_index(lengths, key_pos)[None, :]
    allowed = allowed & (key_pos[None, :] <= query_pos[:, None]) & (key_pos[None, :] >= 0)
    scores = jnp.where(allowed[None], scores, -1e+30)
    top = lax.optimization_barrier(jnp.max(scores, axis=2, keepdims=True))
    raised = jnp.exp(scores - top)
    probs = (raised / lax.optimization_barrier(jnp.sum(raised, axis=2, keepdims=True))).astype(jnp.bfloat16)
    output = jnp.einsum('hqk,khd->qhd', probs.astype(jnp.float32), v_heads)
    return output.reshape(count, heads * width).astype(jnp.bfloat16)

def head_rows(hidden_sum, noise_draws, w_noise, w_out, target, loss_weights):
    count, samples, depth = noise_draws.shape
    lift = jnp.dot(noise_draws.reshape(count * samples, depth), w_noise, preferred_element_type=jnp.float32)
    pre = hidden_sum[:, None, :] + lift.reshape(count, samples, -1)
    act = jax.nn.silu(pre).astype(jnp.bfloat16)
    latent = jnp.dot(act.reshape(count * samples, -1), w_out, preferred_element_type=jnp.float32)
    latent = latent.reshape(count, samples, -1)
    width = latent.shape[2]
    apart = latent[:, :, None, :] - latent[:, None, :, :]
    pair = jnp.sqrt(lax.optimization_barrier(jnp.mean(apart * apart, axis=3)) + EPS)
    others = 1.0 - jnp.eye(samples, dtype=jnp.float32)
    miss = latent - target.astype(jnp.float32)[:, None, :]
    far = jnp.sqrt(lax.optimization_barrier(jnp.mean(miss * miss, axis=2)) + EPS)
    spread = samples * (samples - 1.0)
    losses = 2.0 / samples * lax.optimization_barrier(jnp.sum(far, axis=1)) - lax.optimization_barrier(jnp.sum(pair * others, axis=(1, 2))) / spread
    toward = 2.0 / samples * miss / (width * far[:, :, None])
    repel = 2.0 / spread * lax.optimization_barrier(jnp.sum((others[None] / (width * pair))[:, :, :, None] * apart, axis=2))
    latent_grad = (loss_weights[:, None, None] * (toward - repel)).astype(jnp.bfloat16)
    act_grad = jnp.dot(latent_grad.reshape(count * samples, width), w_out.T, preferred_element_type=jnp.float32)
    act_grad = act_grad.reshape(count, samples, -1)
    sigma = jax.nn.sigmoid(pre)
    pre_grad = act_grad * sigma * (1.0 + pre * (1.0 - sigma))
    return (losses, lax.optimization_barrier(jnp.sum(pre_grad, axis=1)).astype(jnp.bfloat16))

def reference(queries, key_rows, value_rows, lengths, w_first, w_noise, w_out, noise_draws, target, loss_weights):
    margin = NEAR * TOK_DEV
    span = (NEAR + 1) * TOK_DEV
    stacked = jnp.pad(jnp.stack((key_rows, value_rows)), ((0, 0), (margin, 0), (0, 0)))

    def one_block(block):
        start = (block * TOK_DEV).astype(jnp.int32)
        block_queries = lax.dynamic_slice_in_dim(queries, start, TOK_DEV, 0)
        window = lax.dynamic_slice_in_dim(stacked, start, span, 1)
        query_pos = start + jnp.arange(TOK_DEV, dtype=jnp.int32)
        key_pos = start - margin + jnp.arange(span, dtype=jnp.int32)
        return attend(block_queries, window[0], window[1], query_pos, key_pos, lengths, HEADS)
    attended = lax.map(one_block, jnp.arange(BLOCKS, dtype=jnp.int32)).reshape(TOKENS, HEADS * HD)
    hidden_sum = jnp.dot(attended, w_first, preferred_element_type=jnp.float32)

    def head_block(items):
        return head_rows(items[0], items[1], w_noise, w_out, items[2], items[3])
    losses, hidden_grad = lax.map(head_block, (hidden_sum.reshape(BLOCKS, TOK_DEV, -1), noise_draws.reshape(BLOCKS, TOK_DEV, SAMPLES, -1), target.reshape(BLOCKS, TOK_DEV, -1), loss_weights.reshape(BLOCKS, TOK_DEV)))

    def grad_block(total, items):
        part = jnp.dot(items[0].T, items[1], preferred_element_type=jnp.float32).astype(jnp.bfloat16)
        part = lax.optimization_barrier(part)
        return (total + part.astype(jnp.float32), None)
    start_total = jnp.zeros((FFH, HEADS * HD), jnp.float32)
    first_grad, unused = lax.scan(grad_block, start_total, (hidden_grad, attended.reshape(BLOCKS, TOK_DEV, -1)))
    return (attended, losses, first_grad.astype(jnp.bfloat16))
```

```python
import math

import jax
import jax.numpy as jnp
from jax import lax
from jax.sharding import Mesh
from jax.sharding import PartitionSpec as P

HD = 128


EPS = 1e-05


def from_behind(array, axis, by):
    length = lax.axis_size(axis)
    pairs = [(i, i + by) for i in range(length) if 0 <= i + by < length]
    return lax.ppermute(array, axis, pairs)


def doc_index(lengths, positions):
    ends = jnp.cumsum(lengths)
    return jnp.sum((ends[None, :] <= positions[:, None]).astype(jnp.int32), axis=1)


def attend(queries, key_rows, value_rows, query_pos, key_pos, lengths, heads):
    count = queries.shape[0]
    width = queries.shape[1] // heads
    q_heads = queries.reshape(count, heads, width)
    k_heads = key_rows.reshape(-1, heads, width)
    v_heads = value_rows.reshape(-1, heads, width)
    scores = jnp.einsum("qhd,khd->hqk", q_heads, k_heads, preferred_element_type=jnp.float32) * (
        1.0 / math.sqrt(width)
    )
    allowed = doc_index(lengths, query_pos)[:, None] == doc_index(lengths, key_pos)[None, :]
    allowed = allowed & (key_pos[None, :] <= query_pos[:, None]) & (key_pos[None, :] >= 0)
    scores = jnp.where(allowed[None], scores, -1e30)
    top = jnp.max(scores, axis=2, keepdims=True)
    raised = jnp.exp(scores - top)
    probs = (raised / jnp.sum(raised, axis=2, keepdims=True)).astype(jnp.bfloat16)
    output = jnp.einsum("hqk,khd->qhd", probs, v_heads, preferred_element_type=jnp.float32)
    return output.reshape(count, heads * width).astype(jnp.bfloat16)


def head_rows(hidden_sum, noise_draws, w_noise, w_out, target, loss_weights):
    count, samples, depth = noise_draws.shape
    lift = jnp.dot(
        noise_draws.reshape(count * samples, depth), w_noise, preferred_element_type=jnp.float32
    )
    pre = hidden_sum[:, None, :] + lift.reshape(count, samples, -1)
    act = jax.nn.silu(pre).astype(jnp.bfloat16)
    latent = jnp.dot(act.reshape(count * samples, -1), w_out, preferred_element_type=jnp.float32)
    latent = latent.reshape(count, samples, -1)
    width = latent.shape[2]
    apart = latent[:, :, None, :] - latent[:, None, :, :]
    pair = jnp.sqrt(jnp.mean(apart * apart, axis=3) + EPS)
    others = 1.0 - jnp.eye(samples, dtype=jnp.float32)
    miss = latent - target.astype(jnp.float32)[:, None, :]
    far = jnp.sqrt(jnp.mean(miss * miss, axis=2) + EPS)
    spread = samples * (samples - 1.0)
    losses = 2.0 / samples * jnp.sum(far, axis=1) - jnp.sum(pair * others, axis=(1, 2)) / spread
    toward = 2.0 / samples * miss / (width * far[:, :, None])
    repel = 2.0 / spread * jnp.sum((others[None] / (width * pair))[:, :, :, None] * apart, axis=2)
    latent_grad = (loss_weights[:, None, None] * (toward - repel)).astype(jnp.bfloat16)
    act_grad = jnp.dot(
        latent_grad.reshape(count * samples, width), w_out.T, preferred_element_type=jnp.float32
    )
    act_grad = act_grad.reshape(count, samples, -1)
    sigma = jax.nn.sigmoid(pre)
    pre_grad = act_grad * sigma * (1.0 + pre * (1.0 - sigma))
    return (losses, jnp.sum(pre_grad, axis=1).astype(jnp.bfloat16))


def swap(array, axis):
    return lax.ppermute(array, axis, [(0, 1), (1, 0)])


def exchange(array, axis):
    return lax.all_to_all(array, axis, 0, 0, tiled=True)


def shards(
    queries,
    key_rows,
    value_rows,
    lengths,
    w_first,
    w_noise,
    w_out,
    noise_draws,
    target,
    loss_weights,
):
    rows, feat = queries.shape
    heads = feat // HD
    ctx = ("y", "z_hi", "core")
    block_index = lax.axis_index(ctx)
    z_hi, core = lax.axis_index("z_hi"), lax.axis_index("core")
    reach = min(8, lax.axis_size(ctx) // 2)
    stacked = jnp.stack((key_rows, value_rows))
    arrived = []
    moving = stacked
    for step in range(reach):
        moving = from_behind(moving, ctx, 1)
        arrived.append(moving)
    pieces = arrived[::-1]
    pieces.append(stacked)
    window = jnp.concatenate(pieces, axis=1)
    query_pos = block_index * rows + jnp.arange(rows, dtype=jnp.int32)
    key_pos = (block_index - reach) * rows + jnp.arange((reach + 1) * rows, dtype=jnp.int32)
    attended = attend(queries, window[0], window[1], query_pos, key_pos, lengths, heads)

    n_zl, n_x, n_y = (lax.axis_size(name) for name in ("z_lo", "x", "y"))
    n_zh, n_c = lax.axis_size("z_hi"), lax.axis_size("core")
    share = rows // (n_zl * n_x)
    width = w_first.shape[1]

    by_x = attended.reshape(n_zl, n_x, share, feat).transpose(1, 0, 2, 3).reshape(rows, feat)
    partial = jnp.dot(by_x, w_first, preferred_element_type=jnp.float32).astype(jnp.bfloat16)
    partial = exchange(partial, "x").reshape(n_x, n_zl * share, width)
    partial = jnp.sum(partial.astype(jnp.float32), axis=0).astype(jnp.bfloat16)
    partial = exchange(partial, "z_lo").reshape(n_zl, share, width)
    hidden_sum = jnp.sum(partial.astype(jnp.float32), axis=0)

    beside = swap(attended, "core")
    across = swap(attended, "z_hi")
    corner = swap(across, "core")
    near = jnp.where(core == 0, jnp.stack((attended, beside)), jnp.stack((beside, attended)))
    far = jnp.where(core == 0, jnp.stack((across, corner)), jnp.stack((corner, across)))
    group = jnp.where(z_hi == 0, jnp.stack((near, far)), jnp.stack((far, near)))
    group = group.reshape(n_zh, n_c, n_zl, n_x, share, feat).transpose(3, 0, 2, 1, 4, 5)
    group = group.reshape(n_zh * n_c * rows, feat)

    here = lax.axis_index(("z_lo", "x")) * share
    losses_here, grad_here = head_rows(
        hidden_sum,
        lax.dynamic_slice_in_dim(noise_draws, here, share, 0),
        w_noise,
        w_out,
        lax.dynamic_slice_in_dim(target, here, share, 0),
        lax.dynamic_slice_in_dim(loss_weights, here, share, 0),
    )
    part = width // (n_y * n_zh * n_c)
    units = grad_here.reshape(share, n_y, n_zh, n_c, part).transpose(2, 3, 0, 1, 4)
    units = jnp.broadcast_to(units[:, None], (n_zh, n_zl, n_c, share, n_y, part))
    units = exchange(units.reshape(n_zh * n_zl * n_c * share, n_y * part), ("z_hi", "z_lo", "core"))
    units = jnp.broadcast_to(units[None], (n_x,) + units.shape).reshape(-1, n_y * part)
    units = exchange(units, "x")
    carried = lax.dot_general(
        units, group, (((0,), (0,)), ((), ())), preferred_element_type=jnp.float32
    )
    carried = exchange(carried.astype(jnp.bfloat16), "y").reshape(n_y, part, feat)
    first_grad = jnp.sum(carried.astype(jnp.float32), axis=0).astype(jnp.bfloat16)
    return (attended, losses_here[None, :], first_grad)


def solution(mesh):
    sizes = (4, 4, 8, 2, 2)
    fine = Mesh(mesh.devices.reshape(sizes), ("z_lo", "x", "y", "z_hi", "core"))
    ctx, dp = ("y", "z_hi", "core"), ("z_lo", "x")
    placed = (
        P(ctx, dp),
        P(ctx, dp),
        P(ctx, dp),
        P(),
        P(dp, None),
        P(),
        P(),
        P(ctx, None, None),
        P(ctx, None),
        P(ctx),
    )
    return jax.shard_map(
        shards,
        mesh=fine,
        in_specs=placed,
        out_specs=(P(ctx, dp), P(ctx, dp), P(ctx, dp)),
        check_vma=False,
    )
```

```python
import functools
import math

import jax
import jax.numpy as jnp
from jax import lax
from jax.experimental import pallas as pl
from jax.experimental.pallas import tpu as pltpu
from jax.sharding import Mesh
from jax.sharding import PartitionSpec as P

HD = 128
FLOOR = -1e20
MASKED = -1e30


EPS = 1e-05


def attend_kernel(lengths, where, q_ref, here_ref, one_ref, two_ref, *rest, final):
    out_refs, (start_ref, top_ref, total_ref, acc_ref) = rest[:-4], rest[-4:]
    blocks, rows, feat = q_ref.shape
    heads = feat // HD
    scale = 1.4426950408889634 / math.sqrt(HD)
    query = where[0] * rows + lax.broadcasted_iota(jnp.int32, (1, blocks * rows), 1)

    def pass_end(i, carry):
        end, start, first, second = carry
        end = end + lengths[i]
        return (
            end,
            jnp.where(query >= end, end, start),
            jnp.where(where[0] * rows >= end, end, first),
            jnp.where((where[0] + 1) * rows >= end, end, second),
        )

    zero = jnp.int32(0)
    _, start, first, second = lax.fori_loop(
        0, lengths.shape[0], pass_end, (zero, jnp.zeros_like(query), zero, zero)
    )
    for block in range(blocks):
        start_ref[block] = jnp.broadcast_to(start[:, block * rows : (block + 1) * rows], (8, rows))
    top_ref[...] = jnp.full_like(top_ref, FLOOR)
    total_ref[...] = jnp.zeros_like(total_ref)
    acc_ref[...] = jnp.zeros_like(acc_ref)

    for behind, kv_ref in enumerate((here_ref, one_ref, two_ref)):

        def tile(i, carry, behind=behind, kv_ref=kv_ref):
            block, core = i // 2, i % 2
            key_block = where[1] - 4 * behind + core
            query_block = where[0] + block
            lowest = jnp.where(block == 0, first, second)
            live = (key_block <= query_block) & (key_block * rows + rows > lowest)

            @pl.when(live)
            def _():
                key = key_block * rows + lax.broadcasted_iota(jnp.int32, (rows, rows), 0)
                at = query_block * rows + lax.broadcasted_iota(jnp.int32, (rows, rows), 1)
                kept = (key >= start_ref[block, 0:1, :]) & (key <= at)
                for head in range(heads):
                    cols = slice(head * HD, (head + 1) * HD)
                    scores = lax.dot_general(
                        kv_ref[core, 0, :, cols],
                        q_ref[block, :, cols],
                        (((1,), (1,)), ((), ())),
                        preferred_element_type=jnp.float32,
                    )
                    scores = jnp.where(kept, scores * scale, MASKED)
                    old = top_ref[block, head, 0:1, :]
                    top = jnp.maximum(old, jnp.max(scores, axis=0, keepdims=True))
                    raised = jnp.exp2(scores - top)
                    decay = jnp.exp2(old - top)
                    total = total_ref[block, head, 0:1, :] * decay
                    total = total + jnp.sum(raised, axis=0, keepdims=True)
                    product = lax.dot_general(
                        kv_ref[core, 1, :, cols],
                        raised.astype(jnp.bfloat16),
                        (((0,), (0,)), ((), ())),
                        preferred_element_type=jnp.float32,
                    )
                    acc_ref[block, head] = acc_ref[block, head] * decay + product
                    top_ref[block, head] = jnp.broadcast_to(top, (8, rows))
                    total_ref[block, head] = jnp.broadcast_to(total, (8, rows))

            return carry

        lax.fori_loop(0, 2 * blocks, tile, 0)

    for block in range(blocks):
        span = slice(block * rows, (block + 1) * rows)
        for head in range(heads):
            total = total_ref[block, head, 0:1, :]
            some = total > 0.0
            total = jnp.where(some, total, 1.0)
            level = jnp.where(some, top_ref[block, head, 0:1, :] + jnp.log2(total), MASKED)
            values = acc_ref[block, head] * (1.0 / total)
            out_ref = out_refs[0]
            out_ref[head * HD : (head + 1) * HD, span] = values.astype(out_ref.dtype)
            top_ref[block, head, 0:1, :] = level
        if final:
            levels = jnp.concatenate([top_ref[block, head, 0:1, :] for head in range(heads)] * 4, axis=0)
            out_refs[1][:, span] = levels
        else:
            parts = []
            for head in range(heads):
                left = top_ref[block, head, 0:1, :]
                for _ in range(3):
                    part = left.astype(jnp.bfloat16).astype(jnp.float32)
                    parts.append(part)
                    left = left - part
            parts.append(jnp.zeros((16 - 3 * heads, rows), jnp.float32))
            out_refs[0][heads * HD :, span] = jnp.concatenate(parts, axis=0).astype(jnp.bfloat16)


def attend(lengths, where, queries, here, one, two, final):
    blocks, rows, feat = queries.shape
    heads = feat // HD
    if final:
        out = (
            jax.ShapeDtypeStruct((feat, blocks * rows), jnp.float32),
            jax.ShapeDtypeStruct((4 * heads, blocks * rows), jnp.float32),
        )
    else:
        out = (jax.ShapeDtypeStruct((feat + 16, blocks * rows), jnp.bfloat16),)
    smem = pl.BlockSpec(memory_space=pltpu.SMEM)
    vmem = pl.BlockSpec(memory_space=pltpu.VMEM)
    return pl.pallas_call(
        functools.partial(attend_kernel, final=final),
        out_shape=out,
        in_specs=[smem, smem] + [vmem] * 4,
        out_specs=tuple(vmem for _ in out),
        scratch_shapes=[
            pltpu.VMEM((blocks, 8, rows), jnp.int32),
            pltpu.VMEM((blocks, heads, 8, rows), jnp.float32),
            pltpu.VMEM((blocks, heads, 8, rows), jnp.float32),
            pltpu.VMEM((blocks, heads, HD, rows), jnp.float32),
        ],
        compiler_params=pltpu.CompilerParams(vmem_limit_bytes=32 * 1024 * 1024),
        cost_estimate=pl.CostEstimate(
            flops=4 * 9 * rows * rows * feat, bytes_accessed=3 << 20, transcendentals=10 * rows * rows * heads
        ),
        name="attend_own" if final else "attend_across",
    )(lengths, where, queries, here, one, two)


def join_kernel(values_ref, levels_ref, other_ref, out_ref):
    feat, count = values_ref.shape
    for head in range(feat // HD):
        span = slice(head * HD, (head + 1) * HD)
        mine = levels_ref[head : head + 1, :]
        other = other_ref[feat : feat + 16, :].astype(jnp.float32)
        other = other[3 * head : 3 * head + 1] + other[3 * head + 1 : 3 * head + 2] + other[3 * head + 2 : 3 * head + 3]
        top = jnp.maximum(mine, other)
        mine, other = jnp.exp2(mine - top), jnp.exp2(other - top)
        part = 1.0 / (mine + other)
        joined = values_ref[span, :] * (mine * part) + other_ref[span, :].astype(jnp.float32) * (other * part)
        out_ref[:, span] = joined.T.astype(jnp.bfloat16)


def join(values, levels, other):
    feat, count = values.shape
    vmem = pl.BlockSpec(memory_space=pltpu.VMEM)
    return pl.pallas_call(
        join_kernel,
        out_shape=jax.ShapeDtypeStruct((count, feat), jnp.bfloat16),
        in_specs=[vmem] * 3,
        out_specs=vmem,
        compiler_params=pltpu.CompilerParams(vmem_limit_bytes=32 * 1024 * 1024),
        name="join",
    )(values, levels, other)


def head_rows(hidden_sum, noise_draws, w_noise, w_out, target, loss_weights):
    count, samples, depth = noise_draws.shape
    lift = jnp.dot(
        noise_draws.reshape(count * samples, depth), w_noise, preferred_element_type=jnp.float32
    )
    pre = hidden_sum[:, None, :] + lift.reshape(count, samples, -1)
    act = jax.nn.silu(pre).astype(jnp.bfloat16)
    latent = jnp.dot(act.reshape(count * samples, -1), w_out, preferred_element_type=jnp.float32)
    latent = latent.reshape(count, samples, -1)
    width = latent.shape[2]
    apart = latent[:, :, None, :] - latent[:, None, :, :]
    pair = jnp.sqrt(jnp.mean(apart * apart, axis=3) + EPS)
    others = 1.0 - jnp.eye(samples, dtype=jnp.float32)
    miss = latent - target.astype(jnp.float32)[:, None, :]
    far = jnp.sqrt(jnp.mean(miss * miss, axis=2) + EPS)
    spread = samples * (samples - 1.0)
    losses = 2.0 / samples * jnp.sum(far, axis=1) - jnp.sum(pair * others, axis=(1, 2)) / spread
    toward = 2.0 / samples * miss / (width * far[:, :, None])
    repel = 2.0 / spread * jnp.sum((others[None] / (width * pair))[:, :, :, None] * apart, axis=2)
    latent_grad = (loss_weights[:, None, None] * (toward - repel)).astype(jnp.bfloat16)
    act_grad = jnp.dot(
        latent_grad.reshape(count * samples, width), w_out.T, preferred_element_type=jnp.float32
    )
    act_grad = act_grad.reshape(count, samples, -1)
    sigma = jax.nn.sigmoid(pre)
    pre_grad = act_grad * sigma * (1.0 + pre * (1.0 - sigma))
    return (losses, jnp.sum(pre_grad, axis=1).astype(jnp.bfloat16))


def swap(array, axis):
    return lax.ppermute(array, axis, [(0, 1), (1, 0)])


def shift(array, axis):
    length = lax.axis_size(axis)
    return lax.ppermute(array, axis, [(i, (i + 1) % length) for i in range(length)])


def sides(mine, other, core):
    return jnp.where(
        core == 0, jnp.concatenate((mine, other), axis=2), jnp.concatenate((other, mine), axis=2)
    )


def exchange(array, axis):
    return lax.all_to_all(array, axis, 0, 0, tiled=True)


def shards(
    queries,
    key_rows,
    value_rows,
    lengths,
    w_first,
    w_noise,
    w_out,
    noise_draws,
    target,
    loss_weights,
):
    rows, feat = queries.shape
    z_hi, core, y = lax.axis_index("z_hi"), lax.axis_index("core"), lax.axis_index("y")
    half = feat // 2

    kv = jnp.stack((key_rows, value_rows)).reshape(2, rows, 2, half).transpose(2, 0, 1, 3)
    kv = exchange(kv.reshape(4, rows, half), "core").reshape(2, 2, rows, half)
    asked = queries.reshape(rows, 2, half).transpose(1, 0, 2)
    asked = exchange(asked, "core")
    one = shift(kv, "y")
    asked_across = swap(asked, "z_hi")
    two = shift(one, "y")
    base = 4 * y.astype(jnp.int32)
    own, across = base + 2 * z_hi.astype(jnp.int32), base + 2 * (1 - z_hi.astype(jnp.int32))
    sent = attend(lengths, jnp.stack((across, own)), asked_across, kv, one, two, False)[0]
    back = swap(sent, "z_hi")
    values, levels = attend(lengths, jnp.stack((own, own)), asked, kv, one, two, True)
    pair = join(values, levels, back).reshape(2, rows, half)

    pair_across = swap(pair, "z_hi")
    pair_beside = swap(pair, "core")
    near = sides(pair, pair_beside, core)
    attended = lax.dynamic_index_in_dim(near, core, 0, keepdims=False)

    n_zl, n_x, n_y = (lax.axis_size(name) for name in ("z_lo", "x", "y"))
    n_zh, n_c = lax.axis_size("z_hi"), lax.axis_size("core")
    share = rows // (n_zl * n_x)
    width = w_first.shape[1]

    by_x = attended.reshape(n_zl, n_x, share, feat).transpose(1, 0, 2, 3).reshape(rows, feat)
    partial = jnp.dot(by_x, w_first, preferred_element_type=jnp.float32).astype(jnp.bfloat16)
    partial = exchange(partial, "x").reshape(n_x, n_zl * share, width)
    partial = jnp.sum(partial.astype(jnp.float32), axis=0).astype(jnp.bfloat16)
    partial = exchange(partial, "z_lo").reshape(n_zl, share, width)
    hidden_sum = jnp.sum(partial.astype(jnp.float32), axis=0)

    far = sides(pair_across, swap(pair_across, "core"), core)
    group = jnp.where(z_hi == 0, jnp.stack((near, far)), jnp.stack((far, near)))
    group = group.reshape(n_zh, n_c, n_zl, n_x, share, feat).transpose(3, 0, 2, 1, 4, 5)
    group = group.reshape(n_zh * n_c * rows, feat)

    here = lax.axis_index(("z_lo", "x")) * share
    losses_here, grad_here = head_rows(
        hidden_sum,
        lax.dynamic_slice_in_dim(noise_draws, here, share, 0),
        w_noise,
        w_out,
        lax.dynamic_slice_in_dim(target, here, share, 0),
        lax.dynamic_slice_in_dim(loss_weights, here, share, 0),
    )
    part = width // (n_y * n_zh * n_c)
    units = grad_here.reshape(share, n_y, n_zh, n_c, part).transpose(2, 3, 0, 1, 4)
    units = jnp.broadcast_to(units[:, None], (n_zh, n_zl, n_c, share, n_y, part))
    units = exchange(units.reshape(n_zh * n_zl * n_c * share, n_y * part), ("z_hi", "z_lo", "core"))
    units = jnp.broadcast_to(units[None], (n_x,) + units.shape).reshape(-1, n_y * part)
    units = exchange(units, "x")
    carried = lax.dot_general(
        units, group, (((0,), (0,)), ((), ())), preferred_element_type=jnp.float32
    )
    carried = exchange(carried.astype(jnp.bfloat16), "y").reshape(n_y, part, feat)
    first_grad = jnp.sum(carried.astype(jnp.float32), axis=0).astype(jnp.bfloat16)
    return (attended, losses_here[None, :], first_grad)


def solution(mesh):
    sizes = (4, 4, 8, 2, 2)
    fine = Mesh(mesh.devices.reshape(sizes), ("z_lo", "x", "y", "z_hi", "core"))
    ctx, dp = ("y", "z_hi", "core"), ("z_lo", "x")
    placed = (
        P(ctx, dp),
        P(ctx, dp),
        P(ctx, dp),
        P(),
        P(dp, None),
        P(),
        P(),
        P(ctx, None, None),
        P(ctx, None),
        P(ctx),
    )
    return jax.shard_map(
        shards,
        mesh=fine,
        in_specs=placed,
        out_specs=(P(ctx, dp), P(ctx, dp), P(ctx, dp)),
        check_vma=False,
    )
```

```python
import functools
import math

import jax
import jax.numpy as jnp
from jax import lax
from jax.experimental import pallas as pl
from jax.experimental.pallas import tpu as pltpu
from jax.sharding import Mesh
from jax.sharding import PartitionSpec as P

HD = 128
FLOOR = -1e20
MASKED = -1e30


EPS = 1e-05


def attend_kernel(lengths, where, q_ref, *rest, final):
    kv_refs, out_refs = rest[:12], rest[12:-4]
    start_ref, top_ref, total_ref, acc_ref = rest[-4:]
    rows, feat = q_ref.shape
    heads = feat // HD
    scale = 1.4426950408889634 / math.sqrt(HD)
    query_at = where[0] * rows
    query = query_at + lax.broadcasted_iota(jnp.int32, (1, rows), 1)

    def pass_end(i, carry):
        end, start, lowest = carry
        end = end + lengths[i]
        return (end, jnp.where(query >= end, end, start), jnp.where(query_at >= end, end, lowest))

    zero = jnp.int32(0)
    _, start, lowest = lax.fori_loop(
        0, lengths.shape[0], pass_end, (zero, jnp.zeros_like(query), zero)
    )
    start_ref[...] = jnp.broadcast_to(start, start_ref.shape)
    top_ref[...] = jnp.full_like(top_ref, FLOOR)
    total_ref[...] = jnp.zeros_like(total_ref)
    acc_ref[...] = jnp.zeros_like(acc_ref)

    for i in range(6):
        k_ref, v_ref = kv_refs[2 * i], kv_refs[2 * i + 1]
        key_at = (where[1 + i % 2] - 4 * (i // 2)) * rows
        live = (key_at <= query_at) & (key_at + rows > lowest)

        @pl.when(live)
        def _(k_ref=k_ref, v_ref=v_ref, key_at=key_at):
            key = key_at + lax.broadcasted_iota(jnp.int32, (rows, rows), 0)
            at = query_at + lax.broadcasted_iota(jnp.int32, (rows, rows), 1)
            kept = (key >= start_ref[0:1, :]) & (key <= at)

            def two_heads(pair, carry):
                for head in (2 * pair, 2 * pair + 1):
                    cols = pl.ds(pl.multiple_of(head * HD, HD), HD)
                    scores = lax.dot_general(
                        k_ref[:, cols],
                        q_ref[:, cols],
                        (((1,), (1,)), ((), ())),
                        preferred_element_type=jnp.float32,
                    )
                    scores = jnp.where(kept, scores * scale, MASKED)
                    old = top_ref[head, 0:1, :]
                    top = jnp.maximum(old, jnp.max(scores, axis=0, keepdims=True))
                    raised = jnp.exp2(scores - top)
                    decay = jnp.exp2(old - top)
                    total = total_ref[head, 0:1, :] * decay
                    total = total + jnp.sum(raised, axis=0, keepdims=True)
                    product = lax.dot_general(
                        v_ref[:, cols],
                        raised.astype(jnp.bfloat16),
                        (((0,), (0,)), ((), ())),
                        preferred_element_type=jnp.float32,
                    )
                    acc_ref[head] = acc_ref[head] * decay + product
                    top_ref[head] = jnp.broadcast_to(top, (8, rows))
                    total_ref[head] = jnp.broadcast_to(total, (8, rows))
                return carry

            lax.fori_loop(0, heads // 2, two_heads, 0)

    parts = []
    for head in range(heads):
        total = total_ref[head, 0:1, :]
        some = total > 0.0
        total = jnp.where(some, total, 1.0)
        level = jnp.where(some, top_ref[head, 0:1, :] + jnp.log2(total), MASKED)
        values = acc_ref[head] * (1.0 / total)
        out_refs[0][head * HD : (head + 1) * HD, :] = values.astype(out_refs[0].dtype)
        if final:
            parts.append(level)
        else:
            for _ in range(3):
                part = level.astype(jnp.bfloat16).astype(jnp.float32)
                parts.append(part)
                level = level - part
    count = 8 if final else 16
    parts.append(jnp.zeros((count - len(parts), rows), jnp.float32))
    parts = jnp.concatenate(parts, axis=0)
    if final:
        out_refs[1][...] = parts
    else:
        out_refs[0][heads * HD :, :] = parts.astype(jnp.bfloat16)


def attend(lengths, where, queries, kv, final):
    rows, feat = queries.shape
    heads = feat // HD
    if final:
        out = (
            jax.ShapeDtypeStruct((feat, rows), jnp.float32),
            jax.ShapeDtypeStruct((8, rows), jnp.float32),
        )
    else:
        out = (jax.ShapeDtypeStruct((feat + 16, rows), jnp.bfloat16),)
    smem = pl.BlockSpec(memory_space=pltpu.SMEM)
    vmem = pl.BlockSpec(memory_space=pltpu.VMEM)
    return pl.pallas_call(
        functools.partial(attend_kernel, final=final),
        out_shape=out,
        in_specs=[smem, smem] + [vmem] * (1 + len(kv)),
        out_specs=tuple(vmem for _ in out),
        scratch_shapes=[
            pltpu.VMEM((8, rows), jnp.int32),
            pltpu.VMEM((heads, 8, rows), jnp.float32),
            pltpu.VMEM((heads, 8, rows), jnp.float32),
            pltpu.VMEM((heads, HD, rows), jnp.float32),
        ],
        compiler_params=pltpu.CompilerParams(vmem_limit_bytes=16 * 1024 * 1024),
        cost_estimate=pl.CostEstimate(
            flops=4 * 5 * rows * rows * feat, bytes_accessed=3 << 20, transcendentals=5 * rows * rows * heads
        ),
        name="attend_own" if final else "attend_across",
    )(lengths, where, queries, *kv)


def join_kernel(values_ref, levels_ref, other_ref, w_ref, out_ref, partial_ref, order_ref, n_zl):
    feat, count = values_ref.shape
    share = 16
    three = other_ref[feat : feat + 16, :].astype(jnp.float32)
    for head in range(feat // HD):
        span = slice(head * HD, (head + 1) * HD)
        mine = levels_ref[head : head + 1, :]
        other = three[3 * head : 3 * head + 1] + three[3 * head + 1 : 3 * head + 2] + three[3 * head + 2 : 3 * head + 3]
        top = jnp.maximum(mine, other)
        mine, other = jnp.exp2(mine - top), jnp.exp2(other - top)
        part = 1.0 / (mine + other)
        joined = values_ref[span, :] * (mine * part) + other_ref[span, :].astype(jnp.float32) * (other * part)
        out_ref[:, span] = joined.T.astype(jnp.bfloat16)
    n_x = count // share // n_zl
    for x in range(n_x):
        for z in range(n_zl):
            order_ref[pl.ds((x * n_zl + z) * share, share), :] = out_ref[pl.ds((z * n_x + x) * share, share), :]
    width = w_ref.shape[1]
    for at in range(0, width, 512):
        product = jnp.dot(order_ref[...], w_ref[:, at : at + 512], preferred_element_type=jnp.float32)
        partial_ref[:, at : at + 512] = product.astype(jnp.bfloat16)


def join(values, levels, other, w_first, n_zl):
    feat, count = values.shape
    vmem = pl.BlockSpec(memory_space=pltpu.VMEM)
    return pl.pallas_call(
        functools.partial(join_kernel, n_zl=n_zl),
        out_shape=(
            jax.ShapeDtypeStruct((count, feat), jnp.bfloat16),
            jax.ShapeDtypeStruct((count, w_first.shape[1]), jnp.bfloat16),
        ),
        in_specs=[vmem] * 4,
        out_specs=(vmem, vmem),
        scratch_shapes=[pltpu.VMEM((count, feat), jnp.bfloat16)],
        compiler_params=pltpu.CompilerParams(vmem_limit_bytes=16 * 1024 * 1024),
        name="join",
    )(values, levels, other, w_first)


def head_rows(hidden_sum, noise_draws, w_noise, w_out, target, loss_weights):
    count, samples, depth = noise_draws.shape
    lift = jnp.dot(
        noise_draws.reshape(count * samples, depth), w_noise, preferred_element_type=jnp.float32
    )
    pre = hidden_sum[:, None, :] + lift.reshape(count, samples, -1)
    act = jax.nn.silu(pre).astype(jnp.bfloat16)
    latent = jnp.dot(act.reshape(count * samples, -1), w_out, preferred_element_type=jnp.float32)
    latent = latent.reshape(count, samples, -1)
    width = latent.shape[2]
    apart = latent[:, :, None, :] - latent[:, None, :, :]
    pair = jnp.sqrt(jnp.mean(apart * apart, axis=3) + EPS)
    others = 1.0 - jnp.eye(samples, dtype=jnp.float32)
    miss = latent - target.astype(jnp.float32)[:, None, :]
    far = jnp.sqrt(jnp.mean(miss * miss, axis=2) + EPS)
    spread = samples * (samples - 1.0)
    losses = 2.0 / samples * jnp.sum(far, axis=1) - jnp.sum(pair * others, axis=(1, 2)) / spread
    toward = 2.0 / samples * miss / (width * far[:, :, None])
    repel = 2.0 / spread * jnp.sum((others[None] / (width * pair))[:, :, :, None] * apart, axis=2)
    latent_grad = (loss_weights[:, None, None] * (toward - repel)).astype(jnp.bfloat16)
    act_grad = jnp.dot(
        latent_grad.reshape(count * samples, width), w_out.T, preferred_element_type=jnp.float32
    )
    act_grad = act_grad.reshape(count, samples, -1)
    sigma = jax.nn.sigmoid(pre)
    pre_grad = act_grad * sigma * (1.0 + pre * (1.0 - sigma))
    return (losses, jnp.sum(pre_grad, axis=1).astype(jnp.bfloat16))


def swap(array, axis):
    return lax.ppermute(array, axis, [(0, 1), (1, 0)])


def shift(array, axis):
    length = lax.axis_size(axis)
    return lax.ppermute(array, axis, [(i, (i + 1) % length) for i in range(length)])


def exchange(array, axis):
    return lax.all_to_all(array, axis, 0, 0, tiled=True)


def contract_kernel(place, units_ref, mine_ref, other_ref, out_ref, rows_ref, total_ref, n_x, n_zl):
    share = 16
    blocks, count, feat = mine_ref.shape
    for block in range(2 * blocks):
        held_ref = mine_ref if block < blocks else other_ref
        z_hi = place[0] if block % 2 == 0 else 1 - place[0]
        core = place[1] if block < blocks else 1 - place[1]
        for x in range(n_x):
            for z in range(n_zl):
                at = (((x * 2 + z_hi) * n_zl + z) * 2 + core) * share
                rows_ref[pl.ds((z * n_x + x) * share, share), :] = units_ref[pl.ds(pl.multiple_of(at, share), share), :]
        product = lax.dot_general(
            rows_ref[...],
            held_ref[block % blocks],
            (((0,), (0,)), ((), ())),
            preferred_element_type=jnp.float32,
        )
        if block == 0:
            total_ref[...] = product
        else:
            total_ref[...] += product
    out_ref[...] = total_ref[...].astype(jnp.bfloat16)


def contract(place, units, mine, other, n_x, n_zl):
    count, feat = mine.shape[1:]
    width = units.shape[1]
    vmem = pl.BlockSpec(memory_space=pltpu.VMEM)
    return pl.pallas_call(
        functools.partial(contract_kernel, n_x=n_x, n_zl=n_zl),
        out_shape=jax.ShapeDtypeStruct((width, feat), jnp.bfloat16),
        in_specs=[pl.BlockSpec(memory_space=pltpu.SMEM)] + [vmem] * 3,
        out_specs=vmem,
        scratch_shapes=[
            pltpu.VMEM((count, width), jnp.bfloat16),
            pltpu.VMEM((width, feat), jnp.float32),
        ],
        compiler_params=pltpu.CompilerParams(vmem_limit_bytes=32 * 1024 * 1024),
        name="contract",
    )(place, units, mine, other)


def shards(
    queries,
    key_rows,
    value_rows,
    lengths,
    w_first,
    w_noise,
    w_out,
    noise_draws,
    target,
    loss_weights,
):
    rows, feat = queries.shape
    n_zl, n_x, n_y, n_zh, n_c = (
        lax.axis_size(name) for name in ("z_lo", "x", "y", "z_hi", "core")
    )
    y = "y"

    one_k, one_v = shift(key_rows, y), shift(value_rows, y)
    asked = swap(queries, "z_hi")
    two_k, two_v = shift(one_k, y), shift(one_v, y)
    kv = []
    for keys, values in ((key_rows, value_rows), (one_k, one_v), (two_k, two_v)):
        kv += [keys, values, swap(keys, "core"), swap(values, "core")]
    block = lax.axis_index(("y", "z_hi", "core")).astype(jnp.int32)
    beside = block + 1 - 2 * (block % 2)
    across = block + 2 - 4 * (block // 2 % 2)
    sent = attend(lengths, jnp.stack((across, block, beside)), asked, kv, False)[0]
    back = swap(sent, "z_hi")
    values, levels = attend(lengths, jnp.stack((block, block, beside)), queries, kv, True)
    attended, partial = join(values, levels, back, w_first, n_zl)

    share = rows // (n_zl * n_x)
    width = w_first.shape[1]

    over_z = swap(attended, "z_hi")
    partial = exchange(partial, "x").reshape(n_x, n_zl * share, width)
    partial = jnp.sum(partial.astype(jnp.float32), axis=0).astype(jnp.bfloat16)
    partial = exchange(partial, "z_lo").reshape(n_zl, share, width)
    hidden_sum = jnp.sum(partial.astype(jnp.float32), axis=0)

    here = lax.axis_index(("z_lo", "x")) * share
    losses_here, grad_here = head_rows(
        hidden_sum,
        lax.dynamic_slice_in_dim(noise_draws, here, share, 0),
        w_noise,
        w_out,
        lax.dynamic_slice_in_dim(target, here, share, 0),
        lax.dynamic_slice_in_dim(loss_weights, here, share, 0),
    )
    part = width // (n_y * n_zh * n_c)
    units = grad_here.reshape(share, n_y, n_zh, n_c, part).transpose(2, 3, 0, 1, 4)
    units = jnp.broadcast_to(units[:, None], (n_zh, n_zl, n_c, share, n_y, part))
    units = units.reshape(n_zh * n_zl * n_c * share, n_y * part)
    units = exchange(units, ("z_hi", "z_lo", "core"))
    units = jnp.broadcast_to(units[None], (n_x,) + units.shape).reshape(-1, n_y * part)
    mine = jnp.stack((attended, over_z))
    other = swap(mine, "core")
    units = exchange(units, "x")
    place = jnp.stack([lax.axis_index(name) for name in ("z_hi", "core")]).astype(jnp.int32)
    carried = contract(place, units, mine, other, n_x, n_zl)
    carried, losses_here = lax.optimization_barrier((carried, losses_here))
    carried = exchange(carried, "y")
    carried = carried.reshape(n_y, part, feat)
    first_grad = jnp.sum(carried.astype(jnp.float32), axis=0).astype(jnp.bfloat16)
    return (attended, losses_here[None, :], first_grad)


def solution(mesh):
    names = ("z_lo", "x", "y", "z_hi", "core")
    fine = Mesh(mesh.devices.reshape(4, 4, 8, 2, 2), names)
    ctx, dp = names[2:], names[:2]
    placed = (
        P(ctx, dp),
        P(ctx, dp),
        P(ctx, dp),
        P(),
        P(dp, None),
        P(),
        P(),
        P(ctx, None, None),
        P(ctx, None),
        P(ctx),
    )
    return jax.shard_map(
        shards,
        mesh=fine,
        in_specs=placed,
        out_specs=(P(ctx, dp), P(ctx, dp), P(ctx, dp)),
        check_vma=False,
    )
```

```python
import functools
import math

import jax
import jax.numpy as jnp
from jax import lax
from jax.experimental import pallas as pl
from jax.experimental.pallas import tpu as pltpu
from jax.sharding import Mesh
from jax.sharding import PartitionSpec as P

HD = 128
FLOOR = -1e20
MASKED = -1e30


EPS = 1e-05


def attend_kernel(lengths, where, q_ref, *rest, final):
    kv_refs, out_refs = rest[:12], rest[12:-4]
    start_ref, top_ref, total_ref, acc_ref = rest[-4:]
    rows, feat = q_ref.shape
    heads = feat // HD
    scale = 1.4426950408889634 / math.sqrt(HD)
    query_at = where[0] * rows
    query = query_at + lax.broadcasted_iota(jnp.int32, (1, rows), 1)

    def pass_end(i, carry):
        end, start, lowest = carry
        end = end + lengths[i]
        return (end, jnp.where(query >= end, end, start), jnp.where(query_at >= end, end, lowest))

    zero = jnp.int32(0)
    _, start, lowest = lax.fori_loop(
        0, lengths.shape[0], pass_end, (zero, jnp.zeros_like(query), zero)
    )
    start_ref[...] = jnp.broadcast_to(start, start_ref.shape)
    top_ref[...] = jnp.full_like(top_ref, FLOOR)
    total_ref[...] = jnp.zeros_like(total_ref)
    acc_ref[...] = jnp.zeros_like(acc_ref)

    for i in range(6):
        k_ref, v_ref = kv_refs[2 * i], kv_refs[2 * i + 1]
        key_at = (where[1 + i % 2] - 4 * (i // 2)) * rows
        live = (key_at <= query_at) & (key_at + rows > lowest)

        @pl.when(live)
        def _(k_ref=k_ref, v_ref=v_ref, key_at=key_at):
            key = key_at + lax.broadcasted_iota(jnp.int32, (rows, rows), 0)
            at = query_at + lax.broadcasted_iota(jnp.int32, (rows, rows), 1)
            kept = (key >= start_ref[0:1, :]) & (key <= at)

            def two_heads(pair, carry):
                for head in (2 * pair, 2 * pair + 1):
                    cols = pl.ds(pl.multiple_of(head * HD, HD), HD)
                    scores = lax.dot_general(
                        k_ref[:, cols],
                        q_ref[:, cols],
                        (((1,), (1,)), ((), ())),
                        preferred_element_type=jnp.float32,
                    )
                    scores = jnp.where(kept, scores * scale, MASKED)
                    old = top_ref[head, 0:1, :]
                    top = jnp.maximum(old, jnp.max(scores, axis=0, keepdims=True))
                    raised = jnp.exp2(scores - top)
                    decay = jnp.exp2(old - top)
                    total = total_ref[head, 0:1, :] * decay
                    total = total + jnp.sum(raised, axis=0, keepdims=True)
                    product = lax.dot_general(
                        v_ref[:, cols],
                        raised.astype(jnp.bfloat16),
                        (((0,), (0,)), ((), ())),
                        preferred_element_type=jnp.float32,
                    )
                    acc_ref[head] = acc_ref[head] * decay + product
                    top_ref[head] = jnp.broadcast_to(top, (8, rows))
                    total_ref[head] = jnp.broadcast_to(total, (8, rows))
                return carry

            lax.fori_loop(0, heads // 2, two_heads, 0)

    parts = []
    for head in range(heads):
        total = total_ref[head, 0:1, :]
        some = total > 0.0
        total = jnp.where(some, total, 1.0)
        level = jnp.where(some, top_ref[head, 0:1, :] + jnp.log2(total), MASKED)
        values = acc_ref[head] * (1.0 / total)
        out_refs[0][head * HD : (head + 1) * HD, :] = values.astype(out_refs[0].dtype)
        if final:
            parts.append(level)
        else:
            for _ in range(3):
                part = level.astype(jnp.bfloat16).astype(jnp.float32)
                parts.append(part)
                level = level - part
    count = 8 if final else 16
    parts.append(jnp.zeros((count - len(parts), rows), jnp.float32))
    parts = jnp.concatenate(parts, axis=0)
    if final:
        out_refs[1][...] = parts
    else:
        out_refs[0][heads * HD :, :] = parts.astype(jnp.bfloat16)


def attend(lengths, where, queries, kv, final):
    rows, feat = queries.shape
    heads = feat // HD
    if final:
        out = (
            jax.ShapeDtypeStruct((feat, rows), jnp.float32),
            jax.ShapeDtypeStruct((8, rows), jnp.float32),
        )
    else:
        out = (jax.ShapeDtypeStruct((feat + 16, rows), jnp.bfloat16),)
    smem = pl.BlockSpec(memory_space=pltpu.SMEM)
    vmem = pl.BlockSpec(memory_space=pltpu.VMEM)
    return pl.pallas_call(
        functools.partial(attend_kernel, final=final),
        out_shape=out,
        in_specs=[smem, smem] + [vmem] * (1 + len(kv)),
        out_specs=tuple(vmem for _ in out),
        scratch_shapes=[
            pltpu.VMEM((8, rows), jnp.int32),
            pltpu.VMEM((heads, 8, rows), jnp.float32),
            pltpu.VMEM((heads, 8, rows), jnp.float32),
            pltpu.VMEM((heads, HD, rows), jnp.float32),
        ],
        compiler_params=pltpu.CompilerParams(vmem_limit_bytes=16 * 1024 * 1024),
        cost_estimate=pl.CostEstimate(
            flops=4 * 5 * rows * rows * feat, bytes_accessed=3 << 20, transcendentals=5 * rows * rows * heads
        ),
        name="attend_own" if final else "attend_across",
    )(lengths, where, queries, *kv)


def join_kernel(values_ref, levels_ref, other_ref, w_ref, out_ref, partial_ref, order_ref, n_zl):
    feat, count = values_ref.shape
    share = 16
    three = other_ref[feat : feat + 16, :].astype(jnp.float32)
    for head in range(feat // HD):
        span = slice(head * HD, (head + 1) * HD)
        mine = levels_ref[head : head + 1, :]
        other = three[3 * head : 3 * head + 1] + three[3 * head + 1 : 3 * head + 2] + three[3 * head + 2 : 3 * head + 3]
        top = jnp.maximum(mine, other)
        mine, other = jnp.exp2(mine - top), jnp.exp2(other - top)
        part = 1.0 / (mine + other)
        joined = values_ref[span, :] * (mine * part) + other_ref[span, :].astype(jnp.float32) * (other * part)
        out_ref[:, span] = joined.T.astype(jnp.bfloat16)
    n_x = count // share // n_zl
    for x in range(n_x):
        for z in range(n_zl):
            order_ref[pl.ds((x * n_zl + z) * share, share), :] = out_ref[pl.ds((z * n_x + x) * share, share), :]
    width = w_ref.shape[1]
    for at in range(0, width, 512):
        product = jnp.dot(order_ref[...], w_ref[:, at : at + 512], preferred_element_type=jnp.float32)
        partial_ref[:, at : at + 512] = product.astype(jnp.bfloat16)


def join(values, levels, other, w_first, n_zl):
    feat, count = values.shape
    vmem = pl.BlockSpec(memory_space=pltpu.VMEM)
    return pl.pallas_call(
        functools.partial(join_kernel, n_zl=n_zl),
        out_shape=(
            jax.ShapeDtypeStruct((count, feat), jnp.bfloat16),
            jax.ShapeDtypeStruct((count, w_first.shape[1]), jnp.bfloat16),
        ),
        in_specs=[vmem] * 4,
        out_specs=(vmem, vmem),
        scratch_shapes=[pltpu.VMEM((count, feat), jnp.bfloat16)],
        compiler_params=pltpu.CompilerParams(vmem_limit_bytes=16 * 1024 * 1024),
        name="join",
    )(values, levels, other, w_first)


def head_kernel(parts_ref, lift_ref, w_ref, target_ref, weight_ref, losses_ref, units_ref, pre_ref, grad_ref, n_y):
    n_zl, share, width = parts_ref.shape
    count, latents = w_ref.shape[0], w_ref.shape[1]
    samples = lift_ref.shape[0] // share
    step = 512
    latent = jnp.zeros((share * samples, latents), jnp.float32)
    for at in range(0, width, step):
        cols = slice(at, at + step)
        hidden = parts_ref[0, :, cols].astype(jnp.float32)
        for z in range(1, n_zl):
            hidden = hidden + parts_ref[z, :, cols].astype(jnp.float32)
        lift = lift_ref[:, cols].reshape(share, samples, step)
        pre = (hidden[:, None, :] + lift).reshape(share * samples, step)
        pre_ref[:, cols] = pre
        act = (pre * jax.nn.sigmoid(pre)).astype(jnp.bfloat16)
        latent = latent + jnp.dot(act, w_ref[cols, :], preferred_element_type=jnp.float32)
    latent = latent.reshape(share, samples, latents)
    spread = samples * (samples - 1.0)
    pairs = jnp.zeros((share, samples, 1), jnp.float32)
    repel = jnp.zeros_like(latent)
    for by in range(1, samples):
        apart = latent - pltpu.roll(latent, by, 1)
        pair = jnp.sqrt(jnp.mean(apart * apart, axis=2, keepdims=True) + EPS)
        pairs = pairs + pair
        repel = repel + apart * (1.0 / (latents * pair))
    miss = latent - target_ref[...].astype(jnp.float32)[:, None, :]
    far = jnp.sqrt(jnp.mean(miss * miss, axis=2, keepdims=True) + EPS)
    losses = jnp.sum(2.0 / samples * far - pairs / spread, axis=1)
    losses_ref[...] = jnp.broadcast_to(losses, losses_ref.shape)
    toward = 2.0 / samples * miss / (latents * far)
    grad = weight_ref[...][:, None, :] * (toward - 2.0 / spread * repel)
    grad = grad.reshape(share * samples, latents).astype(jnp.bfloat16)
    for at in range(0, width, step):
        cols = slice(at, at + step)
        act_grad = lax.dot_general(
            grad, w_ref[cols, :], (((1,), (1,)), ((), ())), preferred_element_type=jnp.float32
        )
        pre = pre_ref[:, cols]
        sigma = jax.nn.sigmoid(pre)
        pre_grad = act_grad * sigma * (1.0 + pre * (1.0 - sigma))
        grad_ref[:, cols] = jnp.sum(pre_grad.reshape(share, samples, step), axis=1)
    low = lax.broadcasted_iota(jnp.int32, (share, HD), 1) < HD // 2
    for z_hi in range(2):
        for y in range(0, n_y, 2):
            first = grad_ref[:, pl.ds((2 * y + z_hi) * HD, HD)]
            second = grad_ref[:, pl.ds((2 * y + 2 + z_hi) * HD, HD)]
            for core in range(2):
                if core == 0:
                    both = jnp.where(low, first, pltpu.roll(second, HD // 2, 1))
                else:
                    both = jnp.where(low, pltpu.roll(first, HD // 2, 1), second)
                both = both.astype(jnp.bfloat16)
                for z in range(n_zl):
                    row = ((z_hi * n_zl + z) * 2 + core) * share
                    units_ref[row : row + share, y * HD // 2 : y * HD // 2 + HD] = both


def head(parts, lift, w_out, target, weights, n_y):
    n_zl, share, width = parts.shape
    vmem = pl.BlockSpec(memory_space=pltpu.VMEM)
    return pl.pallas_call(
        functools.partial(head_kernel, n_y=n_y),
        out_shape=(
            jax.ShapeDtypeStruct((share, HD), jnp.float32),
            jax.ShapeDtypeStruct((4 * n_zl * share, width // 4), jnp.bfloat16),
        ),
        in_specs=[vmem] * 5,
        out_specs=(vmem, vmem),
        scratch_shapes=[
            pltpu.VMEM((lift.shape[0], width), jnp.float32),
            pltpu.VMEM((share, width), jnp.float32),
        ],
        compiler_params=pltpu.CompilerParams(vmem_limit_bytes=16 * 1024 * 1024),
        name="head",
    )(parts, lift, w_out, target, weights)


def fold_kernel(parts_ref, out_ref):
    total = parts_ref[0].astype(jnp.float32)
    for i in range(1, parts_ref.shape[0]):
        total = total + parts_ref[i].astype(jnp.float32)
    out_ref[...] = total.astype(jnp.bfloat16)


def fold(parts):
    vmem = pl.BlockSpec(memory_space=pltpu.VMEM)
    return pl.pallas_call(
        fold_kernel,
        out_shape=jax.ShapeDtypeStruct(parts.shape[1:], jnp.bfloat16),
        in_specs=[vmem],
        out_specs=vmem,
        compiler_params=pltpu.CompilerParams(vmem_limit_bytes=16 * 1024 * 1024),
        name="fold",
    )(parts)


def repeat_kernel(one_ref, out_ref):
    for i in range(out_ref.shape[0]):
        out_ref[i] = one_ref[...]


def repeat(one, times):
    vmem = pl.BlockSpec(memory_space=pltpu.VMEM)
    return pl.pallas_call(
        repeat_kernel,
        out_shape=jax.ShapeDtypeStruct((times,) + one.shape, one.dtype),
        in_specs=[vmem],
        out_specs=vmem,
        compiler_params=pltpu.CompilerParams(vmem_limit_bytes=16 * 1024 * 1024),
        name="repeat",
    )(one)


def swap(array, axis):
    return lax.ppermute(array, axis, [(0, 1), (1, 0)])


def shift(array, axis):
    length = lax.axis_size(axis)
    return lax.ppermute(array, axis, [(i, (i + 1) % length) for i in range(length)])


def exchange(array, axis):
    return lax.all_to_all(array, axis, 0, 0, tiled=True)


def contract_kernel(place, units_ref, mine_ref, other_ref, out_ref, rows_ref, total_ref, n_x, n_zl):
    share = 16
    blocks, count, feat = mine_ref.shape
    for block in range(2 * blocks):
        held_ref = mine_ref if block < blocks else other_ref
        z_hi = place[0] if block % 2 == 0 else 1 - place[0]
        core = place[1] if block < blocks else 1 - place[1]
        for x in range(n_x):
            for z in range(n_zl):
                at = (((x * 2 + z_hi) * n_zl + z) * 2 + core) * share
                rows_ref[pl.ds((z * n_x + x) * share, share), :] = units_ref[pl.ds(pl.multiple_of(at, share), share), :]
        product = lax.dot_general(
            rows_ref[...],
            held_ref[block % blocks],
            (((0,), (0,)), ((), ())),
            preferred_element_type=jnp.float32,
        )
        if block == 0:
            total_ref[...] = product
        else:
            total_ref[...] += product
    out_ref[...] = total_ref[...].astype(jnp.bfloat16)


def contract(place, units, mine, other, n_x, n_zl):
    count, feat = mine.shape[1:]
    width = units.shape[1]
    vmem = pl.BlockSpec(memory_space=pltpu.VMEM)
    return pl.pallas_call(
        functools.partial(contract_kernel, n_x=n_x, n_zl=n_zl),
        out_shape=jax.ShapeDtypeStruct((width, feat), jnp.bfloat16),
        in_specs=[pl.BlockSpec(memory_space=pltpu.SMEM)] + [vmem] * 3,
        out_specs=vmem,
        scratch_shapes=[
            pltpu.VMEM((count, width), jnp.bfloat16),
            pltpu.VMEM((width, feat), jnp.float32),
        ],
        compiler_params=pltpu.CompilerParams(vmem_limit_bytes=32 * 1024 * 1024),
        name="contract",
    )(place, units, mine, other)


def shards(
    queries,
    key_rows,
    value_rows,
    lengths,
    w_first,
    w_noise,
    w_out,
    noise_draws,
    target,
    loss_weights,
):
    rows, feat = queries.shape
    n_zl, n_x, n_y, n_zh, n_c = (
        lax.axis_size(name) for name in ("z_lo", "x", "y", "z_hi", "core")
    )
    y = "y"

    one_k, one_v = shift(key_rows, y), shift(value_rows, y)
    asked = swap(queries, "z_hi")
    two_k, two_v = shift(one_k, y), shift(one_v, y)
    kv = []
    for keys, values in ((key_rows, value_rows), (one_k, one_v), (two_k, two_v)):
        kv += [keys, values, swap(keys, "core"), swap(values, "core")]
    block = lax.axis_index(("y", "z_hi", "core")).astype(jnp.int32)
    beside = block + 1 - 2 * (block % 2)
    across = block + 2 - 4 * (block // 2 % 2)
    sent = attend(lengths, jnp.stack((across, block, beside)), asked, kv, False)[0]
    back = swap(sent, "z_hi")
    values, levels = attend(lengths, jnp.stack((block, block, beside)), queries, kv, True)
    attended, partial = join(values, levels, back, w_first, n_zl)

    share = rows // (n_zl * n_x)
    width = w_first.shape[1]

    over_z = swap(attended, "z_hi")
    partial = exchange(partial, "x").reshape(n_x, n_zl * share, width)
    partial = exchange(fold(partial), "z_lo").reshape(n_zl, share, width)

    here = lax.axis_index(("z_lo", "x")) * share
    noise = lax.dynamic_slice_in_dim(noise_draws, here, share, 0).reshape(-1, noise_draws.shape[2])
    lift = jnp.dot(noise, w_noise, preferred_element_type=jnp.float32)
    weights = lax.dynamic_slice_in_dim(loss_weights, here, share, 0)
    weights = jnp.broadcast_to(weights[:, None], (share, HD))
    part = width // (n_y * n_zh * n_c)
    losses_here, units = head(
        partial, lift, w_out, lax.dynamic_slice_in_dim(target, here, share, 0), weights, n_y
    )
    losses_here = losses_here[:, 0]
    units = exchange(units, ("z_hi", "z_lo", "core"))
    units = repeat(units, n_x).reshape(-1, n_y * part)
    mine = jnp.stack((attended, over_z))
    other = swap(mine, "core")
    units, other = lax.optimization_barrier((units, other))
    units = exchange(units, "x")
    place = jnp.stack([lax.axis_index(name) for name in ("z_hi", "core")]).astype(jnp.int32)
    carried = contract(place, units, mine, other, n_x, n_zl)
    carried, losses_here = lax.optimization_barrier((carried, losses_here))
    carried = exchange(carried, "y")
    carried = carried.reshape(n_y, part, feat)
    first_grad = jnp.sum(carried.astype(jnp.float32), axis=0).astype(jnp.bfloat16)
    return (attended, losses_here[None, :], first_grad)


def solution(mesh):
    names = ("z_lo", "x", "y", "z_hi", "core")
    fine = Mesh(mesh.devices.reshape(4, 4, 8, 2, 2), names)
    ctx, dp = names[2:], names[:2]
    placed = (
        P(ctx, dp),
        P(ctx, dp),
        P(ctx, dp),
        P(),
        P(dp, None),
        P(),
        P(),
        P(ctx, None, None),
        P(ctx, None),
        P(ctx),
    )
    return jax.shard_map(
        shards,
        mesh=fine,
        in_specs=placed,
        out_specs=(P(ctx, dp), P(ctx, dp), P(ctx, dp)),
        check_vma=False,
    )
```

```python
import functools
import math

import jax
import jax.numpy as jnp
from jax import lax
from jax.experimental import pallas as pl
from jax.experimental.pallas import tpu as pltpu
from jax.sharding import Mesh
from jax.sharding import PartitionSpec as P

HD = 128
FLOOR = -1e20
MASKED = -1e30


EPS = 1e-05


def attend_kernel(lengths, where, q_ref, *rest, final):
    kv_refs, out_refs = rest[:12], rest[12:-4]
    start_ref, top_ref, total_ref, acc_ref = rest[-4:]
    rows, feat = q_ref.shape
    heads = feat // HD
    scale = 1.4426950408889634 / math.sqrt(HD)
    query_at = where[0] * rows
    query = query_at + lax.broadcasted_iota(jnp.int32, (1, rows), 1)

    def pass_end(i, carry):
        end, start, lowest, highest = carry
        end = end + lengths[i]
        return (
            end,
            jnp.where(query >= end, end, start),
            jnp.where(query_at >= end, end, lowest),
            jnp.where(query_at + rows - 1 >= end, end, highest),
        )

    zero = jnp.int32(0)
    _, start, lowest, highest = lax.fori_loop(
        0, lengths.shape[0], pass_end, (zero, jnp.zeros_like(query), zero, zero)
    )
    start_ref[...] = jnp.broadcast_to(start, start_ref.shape)
    top_ref[...] = jnp.full_like(top_ref, FLOOR)
    total_ref[...] = jnp.zeros_like(total_ref)
    acc_ref[...] = jnp.zeros_like(acc_ref)

    def add_tile(k_ref, v_ref, kept):
        for head in range(heads):
            cols = slice(head * HD, (head + 1) * HD)
            scores = lax.dot_general(
                k_ref[:, cols],
                q_ref[:, cols],
                (((1,), (1,)), ((), ())),
                preferred_element_type=jnp.float32,
            )
            scores = scores * scale
            if kept is not None:
                scores = jnp.where(kept, scores, MASKED)
            old = top_ref[head, 0:1, :]
            top = jnp.maximum(old, jnp.max(scores, axis=0, keepdims=True))
            raised = jnp.exp2(scores - top).astype(jnp.bfloat16)
            decay = jnp.exp2(old - top)
            sums = jnp.dot(jnp.ones((16, rows), jnp.bfloat16), raised, preferred_element_type=jnp.float32)
            total = total_ref[head, 0:1, :] * decay + sums[0:1, :]
            product = lax.dot_general(
                v_ref[:, cols],
                raised,
                (((0,), (0,)), ((), ())),
                preferred_element_type=jnp.float32,
            )
            acc_ref[head] = acc_ref[head] * decay + product
            top_ref[head, 0:1, :] = top
            total_ref[head, 0:1, :] = total

    for i in range(6):
        k_ref, v_ref = kv_refs[2 * i], kv_refs[2 * i + 1]
        key_at = (where[1 + i % 2] - 4 * (i // 2)) * rows
        live = (key_at <= query_at) & (key_at + rows > lowest)
        whole = (key_at < query_at) & (key_at >= highest)

        @pl.when(whole)
        def _(k_ref=k_ref, v_ref=v_ref):
            add_tile(k_ref, v_ref, None)

        @pl.when(live & jnp.logical_not(whole))
        def _(k_ref=k_ref, v_ref=v_ref, key_at=key_at):
            key = key_at + lax.broadcasted_iota(jnp.int32, (rows, rows), 0)
            at = query_at + lax.broadcasted_iota(jnp.int32, (rows, rows), 1)
            add_tile(k_ref, v_ref, (key >= start_ref[0:1, :]) & (key <= at))

    parts = []
    for head in range(heads):
        total = total_ref[head, 0:1, :]
        some = total > 0.0
        total = jnp.where(some, total, 1.0)
        level = jnp.where(some, top_ref[head, 0:1, :] + jnp.log2(total), MASKED)
        values = acc_ref[head] * (1.0 / total)
        out_refs[0][head * HD : (head + 1) * HD, :] = values.astype(out_refs[0].dtype)
        if final:
            parts.append(level)
        else:
            for _ in range(3):
                part = level.astype(jnp.bfloat16).astype(jnp.float32)
                parts.append(part)
                level = level - part
    count = 8 if final else 16
    parts.append(jnp.zeros((count - len(parts), rows), jnp.float32))
    parts = jnp.concatenate(parts, axis=0)
    if final:
        out_refs[1][...] = parts
    else:
        out_refs[0][heads * HD :, :] = parts.astype(jnp.bfloat16)


def attend(lengths, where, queries, kv, final):
    rows, feat = queries.shape
    heads = feat // HD
    if final:
        out = (
            jax.ShapeDtypeStruct((feat, rows), jnp.float32),
            jax.ShapeDtypeStruct((8, rows), jnp.float32),
        )
    else:
        out = (jax.ShapeDtypeStruct((feat + 16, rows), jnp.bfloat16),)
    smem = pl.BlockSpec(memory_space=pltpu.SMEM)
    vmem = pl.BlockSpec(memory_space=pltpu.VMEM)
    return pl.pallas_call(
        functools.partial(attend_kernel, final=final),
        out_shape=out,
        in_specs=[smem, smem] + [vmem] * (1 + len(kv)),
        out_specs=tuple(vmem for _ in out),
        scratch_shapes=[
            pltpu.VMEM((8, rows), jnp.int32),
            pltpu.VMEM((heads, 8, rows), jnp.float32),
            pltpu.VMEM((heads, 8, rows), jnp.float32),
            pltpu.VMEM((heads, HD, rows), jnp.float32),
        ],
        compiler_params=pltpu.CompilerParams(vmem_limit_bytes=16 * 1024 * 1024),
        cost_estimate=pl.CostEstimate(
            flops=4 * 5 * rows * rows * feat, bytes_accessed=3 << 20, transcendentals=5 * rows * rows * heads
        ),
        name="attend_own" if final else "attend_across",
    )(lengths, where, queries, *kv)


def join_kernel(values_ref, levels_ref, other_ref, w_ref, out_ref, partial_ref, order_ref, n_zl):
    feat, count = values_ref.shape
    share = 16
    three = other_ref[feat : feat + 16, :].astype(jnp.float32)
    for head in range(feat // HD):
        span = slice(head * HD, (head + 1) * HD)
        mine = levels_ref[head : head + 1, :]
        other = three[3 * head : 3 * head + 1] + three[3 * head + 1 : 3 * head + 2] + three[3 * head + 2 : 3 * head + 3]
        top = jnp.maximum(mine, other)
        mine, other = jnp.exp2(mine - top), jnp.exp2(other - top)
        part = 1.0 / (mine + other)
        joined = values_ref[span, :] * (mine * part) + other_ref[span, :].astype(jnp.float32) * (other * part)
        out_ref[:, span] = joined.T.astype(jnp.bfloat16)
    n_x = count // share // n_zl
    for x in range(n_x):
        for z in range(n_zl):
            order_ref[pl.ds((x * n_zl + z) * share, share), :] = out_ref[pl.ds((z * n_x + x) * share, share), :]
    width = w_ref.shape[1]
    for at in range(0, width, 512):
        product = jnp.dot(order_ref[...], w_ref[:, at : at + 512], preferred_element_type=jnp.float32)
        partial_ref[:, at : at + 512] = product.astype(jnp.bfloat16)


def join(values, levels, other, w_first, n_zl):
    feat, count = values.shape
    vmem = pl.BlockSpec(memory_space=pltpu.VMEM)
    return pl.pallas_call(
        functools.partial(join_kernel, n_zl=n_zl),
        out_shape=(
            jax.ShapeDtypeStruct((count, feat), jnp.bfloat16),
            jax.ShapeDtypeStruct((count, w_first.shape[1]), jnp.bfloat16),
        ),
        in_specs=[vmem] * 4,
        out_specs=(vmem, vmem),
        scratch_shapes=[pltpu.VMEM((count, feat), jnp.bfloat16)],
        compiler_params=pltpu.CompilerParams(vmem_limit_bytes=16 * 1024 * 1024),
        name="join",
    )(values, levels, other, w_first)


def head_kernel(parts_ref, lift_ref, w_ref, target_ref, weight_ref, losses_ref, units_ref, pre_ref, grad_ref, n_y):
    n_zl, share, width = parts_ref.shape
    count, latents = w_ref.shape[0], w_ref.shape[1]
    samples = lift_ref.shape[0] // share
    step = 512
    latent = jnp.zeros((share * samples, latents), jnp.float32)
    for at in range(0, width, step):
        cols = slice(at, at + step)
        hidden = parts_ref[0, :, cols].astype(jnp.float32)
        for z in range(1, n_zl):
            hidden = hidden + parts_ref[z, :, cols].astype(jnp.float32)
        lift = lift_ref[:, cols].reshape(share, samples, step)
        pre = (hidden[:, None, :] + lift).reshape(share * samples, step)
        pre_ref[:, cols] = pre
        act = (pre * jax.nn.sigmoid(pre)).astype(jnp.bfloat16)
        latent = latent + jnp.dot(act, w_ref[cols, :], preferred_element_type=jnp.float32)
    latent = latent.reshape(share, samples, latents)
    spread = samples * (samples - 1.0)
    pairs = jnp.zeros((share, samples, 1), jnp.float32)
    repel = jnp.zeros_like(latent)
    for by in range(1, samples):
        apart = latent - pltpu.roll(latent, by, 1)
        pair = jnp.sqrt(jnp.mean(apart * apart, axis=2, keepdims=True) + EPS)
        pairs = pairs + pair
        repel = repel + apart * (1.0 / (latents * pair))
    miss = latent - target_ref[...].astype(jnp.float32)[:, None, :]
    far = jnp.sqrt(jnp.mean(miss * miss, axis=2, keepdims=True) + EPS)
    losses = jnp.sum(2.0 / samples * far - pairs / spread, axis=1)
    losses_ref[...] = jnp.broadcast_to(losses, losses_ref.shape)
    toward = 2.0 / samples * miss / (latents * far)
    grad = weight_ref[...][:, None, :] * (toward - 2.0 / spread * repel)
    grad = grad.reshape(share * samples, latents).astype(jnp.bfloat16)
    for at in range(0, width, step):
        cols = slice(at, at + step)
        act_grad = lax.dot_general(
            grad, w_ref[cols, :], (((1,), (1,)), ((), ())), preferred_element_type=jnp.float32
        )
        pre = pre_ref[:, cols]
        sigma = jax.nn.sigmoid(pre)
        pre_grad = act_grad * sigma * (1.0 + pre * (1.0 - sigma))
        grad_ref[:, cols] = jnp.sum(pre_grad.reshape(share, samples, step), axis=1)
    low = lax.broadcasted_iota(jnp.int32, (share, HD), 1) < HD // 2
    for z_hi in range(2):
        for y in range(0, n_y, 2):
            first = grad_ref[:, pl.ds((2 * y + z_hi) * HD, HD)]
            second = grad_ref[:, pl.ds((2 * y + 2 + z_hi) * HD, HD)]
            for core in range(2):
                if core == 0:
                    both = jnp.where(low, first, pltpu.roll(second, HD // 2, 1))
                else:
                    both = jnp.where(low, pltpu.roll(first, HD // 2, 1), second)
                both = both.astype(jnp.bfloat16)
                for z in range(n_zl):
                    row = ((z_hi * n_zl + z) * 2 + core) * share
                    units_ref[row : row + share, y * HD // 2 : y * HD // 2 + HD] = both


def head(parts, lift, w_out, target, weights, n_y):
    n_zl, share, width = parts.shape
    vmem = pl.BlockSpec(memory_space=pltpu.VMEM)
    return pl.pallas_call(
        functools.partial(head_kernel, n_y=n_y),
        out_shape=(
            jax.ShapeDtypeStruct((share, HD), jnp.float32),
            jax.ShapeDtypeStruct((4 * n_zl * share, width // 4), jnp.bfloat16),
        ),
        in_specs=[vmem] * 5,
        out_specs=(vmem, vmem),
        scratch_shapes=[
            pltpu.VMEM((lift.shape[0], width), jnp.float32),
            pltpu.VMEM((share, width), jnp.float32),
        ],
        compiler_params=pltpu.CompilerParams(vmem_limit_bytes=16 * 1024 * 1024),
        name="head",
    )(parts, lift, w_out, target, weights)


def fold_kernel(parts_ref, out_ref):
    total = parts_ref[0].astype(jnp.float32)
    for i in range(1, parts_ref.shape[0]):
        total = total + parts_ref[i].astype(jnp.float32)
    out_ref[...] = total.astype(jnp.bfloat16)


def fold(parts):
    vmem = pl.BlockSpec(memory_space=pltpu.VMEM)
    return pl.pallas_call(
        fold_kernel,
        out_shape=jax.ShapeDtypeStruct(parts.shape[1:], jnp.bfloat16),
        in_specs=[vmem],
        out_specs=vmem,
        compiler_params=pltpu.CompilerParams(vmem_limit_bytes=16 * 1024 * 1024),
        name="fold",
    )(parts)


def repeat_kernel(one_ref, out_ref):
    for i in range(out_ref.shape[0]):
        out_ref[i] = one_ref[...]


def repeat(one, times):
    vmem = pl.BlockSpec(memory_space=pltpu.VMEM)
    return pl.pallas_call(
        repeat_kernel,
        out_shape=jax.ShapeDtypeStruct((times,) + one.shape, one.dtype),
        in_specs=[vmem],
        out_specs=vmem,
        compiler_params=pltpu.CompilerParams(vmem_limit_bytes=16 * 1024 * 1024),
        name="repeat",
    )(one)


def swap(array, axis):
    return lax.ppermute(array, axis, [(0, 1), (1, 0)])


def shift(array, axis):
    length = lax.axis_size(axis)
    return lax.ppermute(array, axis, [(i, (i + 1) % length) for i in range(length)])


def exchange(array, axis):
    return lax.all_to_all(array, axis, 0, 0, tiled=True)


def contract_kernel(place, units_ref, mine_ref, other_ref, out_ref, rows_ref, total_ref, n_x, n_zl):
    share = 16
    blocks, count, feat = mine_ref.shape
    for block in range(2 * blocks):
        held_ref = mine_ref if block < blocks else other_ref
        z_hi = place[0] if block % 2 == 0 else 1 - place[0]
        core = place[1] if block < blocks else 1 - place[1]
        for x in range(n_x):
            for z in range(n_zl):
                at = (((x * 2 + z_hi) * n_zl + z) * 2 + core) * share
                rows_ref[pl.ds((z * n_x + x) * share, share), :] = units_ref[pl.ds(pl.multiple_of(at, share), share), :]
        product = lax.dot_general(
            rows_ref[...],
            held_ref[block % blocks],
            (((0,), (0,)), ((), ())),
            preferred_element_type=jnp.float32,
        )
        if block == 0:
            total_ref[...] = product
        else:
            total_ref[...] += product
    out_ref[...] = total_ref[...].astype(jnp.bfloat16)


def contract(place, units, mine, other, n_x, n_zl):
    count, feat = mine.shape[1:]
    width = units.shape[1]
    vmem = pl.BlockSpec(memory_space=pltpu.VMEM)
    return pl.pallas_call(
        functools.partial(contract_kernel, n_x=n_x, n_zl=n_zl),
        out_shape=jax.ShapeDtypeStruct((width, feat), jnp.bfloat16),
        in_specs=[pl.BlockSpec(memory_space=pltpu.SMEM)] + [vmem] * 3,
        out_specs=vmem,
        scratch_shapes=[
            pltpu.VMEM((count, width), jnp.bfloat16),
            pltpu.VMEM((width, feat), jnp.float32),
        ],
        compiler_params=pltpu.CompilerParams(vmem_limit_bytes=32 * 1024 * 1024),
        name="contract",
    )(place, units, mine, other)


def shards(
    queries,
    key_rows,
    value_rows,
    lengths,
    w_first,
    w_noise,
    w_out,
    noise_draws,
    target,
    loss_weights,
):
    rows, feat = queries.shape
    n_zl, n_x, n_y, n_zh, n_c = (
        lax.axis_size(name) for name in ("z_lo", "x", "y", "z_hi", "core")
    )
    y = "y"

    one_k, one_v = shift(key_rows, y), shift(value_rows, y)
    asked = swap(queries, "z_hi")
    two_k, two_v = shift(one_k, y), shift(one_v, y)
    kv = []
    for keys, values in ((key_rows, value_rows), (one_k, one_v), (two_k, two_v)):
        kv += [keys, values, swap(keys, "core"), swap(values, "core")]
    block = lax.axis_index(("y", "z_hi", "core")).astype(jnp.int32)
    beside = block + 1 - 2 * (block % 2)
    across = block + 2 - 4 * (block // 2 % 2)
    sent = attend(lengths, jnp.stack((across, block, beside)), asked, kv, False)[0]
    back = swap(sent, "z_hi")
    values, levels = attend(lengths, jnp.stack((block, block, beside)), queries, kv, True)
    attended, partial = join(values, levels, back, w_first, n_zl)

    share = rows // (n_zl * n_x)
    width = w_first.shape[1]

    over_z = swap(attended, "z_hi")
    partial = exchange(partial, "x").reshape(n_x, n_zl * share, width)
    partial = exchange(fold(partial), "z_lo").reshape(n_zl, share, width)

    here = lax.axis_index(("z_lo", "x")) * share
    noise = lax.dynamic_slice_in_dim(noise_draws, here, share, 0).reshape(-1, noise_draws.shape[2])
    lift = jnp.dot(noise, w_noise, preferred_element_type=jnp.float32)
    weights = lax.dynamic_slice_in_dim(loss_weights, here, share, 0)
    weights = jnp.broadcast_to(weights[:, None], (share, HD))
    part = width // (n_y * n_zh * n_c)
    losses_here, units = head(
        partial, lift, w_out, lax.dynamic_slice_in_dim(target, here, share, 0), weights, n_y
    )
    losses_here = losses_here[:, 0]
    units = exchange(units, ("z_hi", "z_lo", "core"))
    units = repeat(units, n_x).reshape(-1, n_y * part)
    mine = jnp.stack((attended, over_z))
    other = swap(mine, "core")
    units, other = lax.optimization_barrier((units, other))
    units = exchange(units, "x")
    place = jnp.stack([lax.axis_index(name) for name in ("z_hi", "core")]).astype(jnp.int32)
    carried = contract(place, units, mine, other, n_x, n_zl)
    carried, losses_here = lax.optimization_barrier((carried, losses_here))
    carried = exchange(carried, "y")
    carried = carried.reshape(n_y, part, feat)
    first_grad = jnp.sum(carried.astype(jnp.float32), axis=0).astype(jnp.bfloat16)
    return (attended, losses_here[None, :], first_grad)


def solution(mesh):
    names = ("z_lo", "x", "y", "z_hi", "core")
    fine = Mesh(mesh.devices.reshape(4, 4, 8, 2, 2), names)
    ctx, dp = names[2:], names[:2]
    placed = (
        P(ctx, dp),
        P(ctx, dp),
        P(ctx, dp),
        P(),
        P(dp, None),
        P(),
        P(),
        P(ctx, None, None),
        P(ctx, None),
        P(ctx),
    )
    return jax.shard_map(
        shards,
        mesh=fine,
        in_specs=placed,
        out_specs=(P(ctx, dp), P(ctx, dp), P(ctx, dp)),
        check_vma=False,
    )
```

```python
import functools
import math

import jax
import jax.numpy as jnp
from jax import lax
from jax.experimental import pallas as pl
from jax.experimental.pallas import tpu as pltpu
from jax.sharding import Mesh
from jax.sharding import PartitionSpec as P

HD = 128
FLOOR = -1e20
MASKED = -1e30


EPS = 1e-05


def attend_kernel(lengths, where, q_ref, *rest, final):
    kv_refs, out_refs = rest[:12], rest[12:-4]
    start_ref, top_ref, total_ref, acc_ref = rest[-4:]
    rows, feat = q_ref.shape
    heads = feat // HD
    scale = 1.4426950408889634 / math.sqrt(HD)
    query_at = where[0] * rows
    query = query_at + lax.broadcasted_iota(jnp.int32, (1, rows), 1)

    def pass_end(i, carry):
        end, start, lowest, highest = carry
        end = end + lengths[i]
        return (
            end,
            jnp.where(query >= end, end, start),
            jnp.where(query_at >= end, end, lowest),
            jnp.where(query_at + rows - 1 >= end, end, highest),
        )

    zero = jnp.int32(0)
    _, start, lowest, highest = lax.fori_loop(
        0, lengths.shape[0], pass_end, (zero, jnp.zeros_like(query), zero, zero), unroll=16
    )
    start_ref[...] = jnp.broadcast_to(start, start_ref.shape)
    top_ref[...] = jnp.full_like(top_ref, FLOOR)
    total_ref[...] = jnp.zeros_like(total_ref)
    acc_ref[...] = jnp.zeros_like(acc_ref)

    def add_tile(k_ref, v_ref, kept):
        for head in range(heads):
            cols = slice(head * HD, (head + 1) * HD)
            scores = lax.dot_general(
                k_ref[:, cols],
                q_ref[:, cols],
                (((1,), (1,)), ((), ())),
                preferred_element_type=jnp.float32,
            )
            scores = scores * scale
            if kept is not None:
                scores = jnp.where(kept, scores, MASKED)
            old = top_ref[head, 0:1, :]
            top = jnp.maximum(old, jnp.max(scores, axis=0, keepdims=True))
            raised = jnp.exp2(scores - top).astype(jnp.bfloat16)
            decay = jnp.exp2(old - top)
            sums = jnp.dot(jnp.ones((16, rows), jnp.bfloat16), raised, preferred_element_type=jnp.float32)
            total = total_ref[head, 0:1, :] * decay + sums[0:1, :]
            product = lax.dot_general(
                v_ref[:, cols],
                raised,
                (((0,), (0,)), ((), ())),
                preferred_element_type=jnp.float32,
            )
            acc_ref[head] = acc_ref[head] * decay + product
            top_ref[head, 0:1, :] = top
            total_ref[head, 0:1, :] = total

    for i in range(6):
        k_ref, v_ref = kv_refs[2 * i], kv_refs[2 * i + 1]
        key_at = (where[1 + i % 2] - 4 * (i // 2)) * rows
        live = (key_at <= query_at) & (key_at + rows > lowest)
        whole = (key_at < query_at) & (key_at >= highest)

        @pl.when(whole)
        def _(k_ref=k_ref, v_ref=v_ref):
            add_tile(k_ref, v_ref, None)

        @pl.when(live & jnp.logical_not(whole))
        def _(k_ref=k_ref, v_ref=v_ref, key_at=key_at):
            key = key_at + lax.broadcasted_iota(jnp.int32, (rows, rows), 0)
            at = query_at + lax.broadcasted_iota(jnp.int32, (rows, rows), 1)
            add_tile(k_ref, v_ref, (key >= start_ref[0:1, :]) & (key <= at))

    parts = []
    for head in range(heads):
        total = total_ref[head, 0:1, :]
        some = total > 0.0
        total = jnp.where(some, total, 1.0)
        level = jnp.where(some, top_ref[head, 0:1, :] + jnp.log2(total), MASKED)
        values = acc_ref[head] * (1.0 / total)
        out_refs[0][head * HD : (head + 1) * HD, :] = values.astype(out_refs[0].dtype)
        if final:
            parts.append(level)
        else:
            for _ in range(3):
                part = level.astype(jnp.bfloat16).astype(jnp.float32)
                parts.append(part)
                level = level - part
    count = 8 if final else 16
    parts.append(jnp.zeros((count - len(parts), rows), jnp.float32))
    parts = jnp.concatenate(parts, axis=0)
    if final:
        out_refs[1][...] = parts
    else:
        out_refs[0][heads * HD :, :] = parts.astype(jnp.bfloat16)


def attend(lengths, where, queries, kv, final):
    rows, feat = queries.shape
    heads = feat // HD
    if final:
        out = (
            jax.ShapeDtypeStruct((feat, rows), jnp.float32),
            jax.ShapeDtypeStruct((8, rows), jnp.float32),
        )
    else:
        out = (jax.ShapeDtypeStruct((feat + 16, rows), jnp.bfloat16),)
    smem = pl.BlockSpec(memory_space=pltpu.SMEM)
    vmem = pl.BlockSpec(memory_space=pltpu.VMEM)
    return pl.pallas_call(
        functools.partial(attend_kernel, final=final),
        out_shape=out,
        in_specs=[smem, smem] + [vmem] * (1 + len(kv)),
        out_specs=tuple(vmem for _ in out),
        scratch_shapes=[
            pltpu.VMEM((8, rows), jnp.int32),
            pltpu.VMEM((heads, 8, rows), jnp.float32),
            pltpu.VMEM((heads, 8, rows), jnp.float32),
            pltpu.VMEM((heads, HD, rows), jnp.float32),
        ],
        compiler_params=pltpu.CompilerParams(vmem_limit_bytes=16 * 1024 * 1024),
        cost_estimate=pl.CostEstimate(
            flops=4 * 5 * rows * rows * feat, bytes_accessed=3 << 20, transcendentals=5 * rows * rows * heads
        ),
        name="attend_own" if final else "attend_across",
    )(lengths, where, queries, *kv)


def join_kernel(values_ref, levels_ref, other_ref, w_ref, out_ref, partial_ref, order_ref, n_zl):
    feat, count = values_ref.shape
    share = 16
    three = other_ref[feat : feat + 16, :].astype(jnp.float32)
    for head in range(feat // HD):
        span = slice(head * HD, (head + 1) * HD)
        mine = levels_ref[head : head + 1, :]
        other = three[3 * head : 3 * head + 1] + three[3 * head + 1 : 3 * head + 2] + three[3 * head + 2 : 3 * head + 3]
        top = jnp.maximum(mine, other)
        mine, other = jnp.exp2(mine - top), jnp.exp2(other - top)
        part = 1.0 / (mine + other)
        joined = values_ref[span, :] * (mine * part) + other_ref[span, :].astype(jnp.float32) * (other * part)
        out_ref[:, span] = joined.T.astype(jnp.bfloat16)
    n_x = count // share // n_zl
    for x in range(n_x):
        for z in range(n_zl):
            order_ref[pl.ds((x * n_zl + z) * share, share), :] = out_ref[pl.ds((z * n_x + x) * share, share), :]
    width = w_ref.shape[1]
    for at in range(0, width, 512):
        product = jnp.dot(order_ref[...], w_ref[:, at : at + 512], preferred_element_type=jnp.float32)
        partial_ref[:, at : at + 512] = product.astype(jnp.bfloat16)


def join(values, levels, other, w_first, n_zl):
    feat, count = values.shape
    vmem = pl.BlockSpec(memory_space=pltpu.VMEM)
    return pl.pallas_call(
        functools.partial(join_kernel, n_zl=n_zl),
        out_shape=(
            jax.ShapeDtypeStruct((count, feat), jnp.bfloat16),
            jax.ShapeDtypeStruct((count, w_first.shape[1]), jnp.bfloat16),
        ),
        in_specs=[vmem] * 4,
        out_specs=(vmem, vmem),
        scratch_shapes=[pltpu.VMEM((count, feat), jnp.bfloat16)],
        compiler_params=pltpu.CompilerParams(vmem_limit_bytes=16 * 1024 * 1024),
        name="join",
    )(values, levels, other, w_first)


def head_kernel(parts_ref, lift_ref, w_ref, target_ref, weight_ref, losses_ref, units_ref, pre_ref, grad_ref, n_y):
    n_zl, share, width = parts_ref.shape
    count, latents = w_ref.shape[0], w_ref.shape[1]
    samples = lift_ref.shape[0] // share
    step = 512
    latent = jnp.zeros((share * samples, latents), jnp.float32)
    for at in range(0, width, step):
        cols = slice(at, at + step)
        hidden = parts_ref[0, :, cols].astype(jnp.float32)
        for z in range(1, n_zl):
            hidden = hidden + parts_ref[z, :, cols].astype(jnp.float32)
        lift = lift_ref[:, cols].reshape(share, samples, step)
        pre = (hidden[:, None, :] + lift).reshape(share * samples, step)
        pre_ref[:, cols] = pre
        act = (pre * jax.nn.sigmoid(pre)).astype(jnp.bfloat16)
        latent = latent + jnp.dot(act, w_ref[cols, :], preferred_element_type=jnp.float32)
    latent = latent.reshape(share, samples, latents)
    spread = samples * (samples - 1.0)
    pairs = jnp.zeros((share, samples, 1), jnp.float32)
    repel = jnp.zeros_like(latent)
    for by in range(1, samples):
        apart = latent - pltpu.roll(latent, by, 1)
        pair = jnp.sqrt(jnp.mean(apart * apart, axis=2, keepdims=True) + EPS)
        pairs = pairs + pair
        repel = repel + apart * (1.0 / (latents * pair))
    miss = latent - target_ref[...].astype(jnp.float32)[:, None, :]
    far = jnp.sqrt(jnp.mean(miss * miss, axis=2, keepdims=True) + EPS)
    losses = jnp.sum(2.0 / samples * far - pairs / spread, axis=1)
    losses_ref[...] = jnp.broadcast_to(losses, losses_ref.shape)
    toward = 2.0 / samples * miss / (latents * far)
    grad = weight_ref[...][:, None, :] * (toward - 2.0 / spread * repel)
    grad = grad.reshape(share * samples, latents).astype(jnp.bfloat16)
    for at in range(0, width, step):
        cols = slice(at, at + step)
        act_grad = lax.dot_general(
            grad, w_ref[cols, :], (((1,), (1,)), ((), ())), preferred_element_type=jnp.float32
        )
        pre = pre_ref[:, cols]
        sigma = jax.nn.sigmoid(pre)
        pre_grad = act_grad * sigma * (1.0 + pre * (1.0 - sigma))
        grad_ref[:, cols] = jnp.sum(pre_grad.reshape(share, samples, step), axis=1)
    low = lax.broadcasted_iota(jnp.int32, (share, HD), 1) < HD // 2
    for z_hi in range(2):
        for y in range(0, n_y, 2):
            first = grad_ref[:, pl.ds((2 * y + z_hi) * HD, HD)]
            second = grad_ref[:, pl.ds((2 * y + 2 + z_hi) * HD, HD)]
            for core in range(2):
                if core == 0:
                    both = jnp.where(low, first, pltpu.roll(second, HD // 2, 1))
                else:
                    both = jnp.where(low, pltpu.roll(first, HD // 2, 1), second)
                both = both.astype(jnp.bfloat16)
                for z in range(n_zl):
                    row = ((z_hi * n_zl + z) * 2 + core) * share
                    units_ref[row : row + share, y * HD // 2 : y * HD // 2 + HD] = both


def head(parts, lift, w_out, target, weights, n_y):
    n_zl, share, width = parts.shape
    vmem = pl.BlockSpec(memory_space=pltpu.VMEM)
    return pl.pallas_call(
        functools.partial(head_kernel, n_y=n_y),
        out_shape=(
            jax.ShapeDtypeStruct((share, HD), jnp.float32),
            jax.ShapeDtypeStruct((4 * n_zl * share, width // 4), jnp.bfloat16),
        ),
        in_specs=[vmem] * 5,
        out_specs=(vmem, vmem),
        scratch_shapes=[
            pltpu.VMEM((lift.shape[0], width), jnp.float32),
            pltpu.VMEM((share, width), jnp.float32),
        ],
        compiler_params=pltpu.CompilerParams(vmem_limit_bytes=16 * 1024 * 1024),
        name="head",
    )(parts, lift, w_out, target, weights)


def fold_kernel(parts_ref, out_ref):
    total = parts_ref[0].astype(jnp.float32)
    for i in range(1, parts_ref.shape[0]):
        total = total + parts_ref[i].astype(jnp.float32)
    out_ref[...] = total.astype(jnp.bfloat16)


def fold(parts):
    vmem = pl.BlockSpec(memory_space=pltpu.VMEM)
    return pl.pallas_call(
        fold_kernel,
        out_shape=jax.ShapeDtypeStruct(parts.shape[1:], jnp.bfloat16),
        in_specs=[vmem],
        out_specs=vmem,
        compiler_params=pltpu.CompilerParams(vmem_limit_bytes=16 * 1024 * 1024),
        name="fold",
    )(parts)


def repeat_kernel(one_ref, out_ref):
    for i in range(out_ref.shape[0]):
        out_ref[i] = one_ref[...]


def repeat(one, times):
    vmem = pl.BlockSpec(memory_space=pltpu.VMEM)
    return pl.pallas_call(
        repeat_kernel,
        out_shape=jax.ShapeDtypeStruct((times,) + one.shape, one.dtype),
        in_specs=[vmem],
        out_specs=vmem,
        compiler_params=pltpu.CompilerParams(vmem_limit_bytes=16 * 1024 * 1024),
        name="repeat",
    )(one)


def swap(array, axis):
    return lax.ppermute(array, axis, [(0, 1), (1, 0)])


def shift(array, axis):
    length = lax.axis_size(axis)
    return lax.ppermute(array, axis, [(i, (i + 1) % length) for i in range(length)])


def exchange(array, axis):
    return lax.all_to_all(array, axis, 0, 0, tiled=True)


def contract_kernel(place, units_ref, mine_ref, other_ref, out_ref, rows_ref, total_ref, n_x, n_zl):
    share = 16
    blocks, count, feat = mine_ref.shape
    for block in range(2 * blocks):
        held_ref = mine_ref if block < blocks else other_ref
        z_hi = place[0] if block % 2 == 0 else 1 - place[0]
        core = place[1] if block < blocks else 1 - place[1]
        for x in range(n_x):
            for z in range(n_zl):
                at = (((x * 2 + z_hi) * n_zl + z) * 2 + core) * share
                rows_ref[pl.ds((z * n_x + x) * share, share), :] = units_ref[pl.ds(pl.multiple_of(at, share), share), :]
        product = lax.dot_general(
            rows_ref[...],
            held_ref[block % blocks],
            (((0,), (0,)), ((), ())),
            preferred_element_type=jnp.float32,
        )
        if block == 0:
            total_ref[...] = product
        else:
            total_ref[...] += product
    out_ref[...] = total_ref[...].astype(jnp.bfloat16)


def contract(place, units, mine, other, n_x, n_zl):
    count, feat = mine.shape[1:]
    width = units.shape[1]
    vmem = pl.BlockSpec(memory_space=pltpu.VMEM)
    return pl.pallas_call(
        functools.partial(contract_kernel, n_x=n_x, n_zl=n_zl),
        out_shape=jax.ShapeDtypeStruct((width, feat), jnp.bfloat16),
        in_specs=[pl.BlockSpec(memory_space=pltpu.SMEM)] + [vmem] * 3,
        out_specs=vmem,
        scratch_shapes=[
            pltpu.VMEM((count, width), jnp.bfloat16),
            pltpu.VMEM((width, feat), jnp.float32),
        ],
        compiler_params=pltpu.CompilerParams(vmem_limit_bytes=32 * 1024 * 1024),
        name="contract",
    )(place, units, mine, other)


def shards(
    queries,
    key_rows,
    value_rows,
    lengths,
    w_first,
    w_noise,
    w_out,
    noise_draws,
    target,
    loss_weights,
):
    rows, feat = queries.shape
    n_zl, n_x, n_y, n_zh, n_c = (
        lax.axis_size(name) for name in ("z_lo", "x", "y", "z_hi", "core")
    )
    y = "y"

    one_k, one_v = shift(key_rows, y), shift(value_rows, y)
    asked = swap(queries, "z_hi")
    two_k, two_v = shift(one_k, y), shift(one_v, y)
    kv = []
    for keys, values in ((key_rows, value_rows), (one_k, one_v), (two_k, two_v)):
        kv += [keys, values, swap(keys, "core"), swap(values, "core")]
    block = lax.axis_index(("y", "z_hi", "core")).astype(jnp.int32)
    beside = block + 1 - 2 * (block % 2)
    across = block + 2 - 4 * (block // 2 % 2)
    sent = attend(lengths, jnp.stack((across, block, beside)), asked, kv, False)[0]
    back = swap(sent, "z_hi")
    values, levels = attend(lengths, jnp.stack((block, block, beside)), queries, kv, True)
    attended, partial = join(values, levels, back, w_first, n_zl)

    share = rows // (n_zl * n_x)
    width = w_first.shape[1]

    over_z = swap(attended, "z_hi")
    partial = exchange(partial, "x").reshape(n_x, n_zl * share, width)
    partial = exchange(fold(partial), "z_lo").reshape(n_zl, share, width)

    here = lax.axis_index(("z_lo", "x")) * share
    noise = lax.dynamic_slice_in_dim(noise_draws, here, share, 0).reshape(-1, noise_draws.shape[2])
    lift = jnp.dot(noise, w_noise, preferred_element_type=jnp.float32)
    weights = lax.dynamic_slice_in_dim(loss_weights, here, share, 0)
    weights = jnp.broadcast_to(weights[:, None], (share, HD))
    part = width // (n_y * n_zh * n_c)
    losses_here, units = head(
        partial, lift, w_out, lax.dynamic_slice_in_dim(target, here, share, 0), weights, n_y
    )
    losses_here = losses_here[:, 0]
    units = exchange(units, ("z_hi", "z_lo", "core"))
    units = repeat(units, n_x).reshape(-1, n_y * part)
    mine = jnp.stack((attended, over_z))
    other = swap(mine, "core")
    units, other = lax.optimization_barrier((units, other))
    units = exchange(units, "x")
    place = jnp.stack([lax.axis_index(name) for name in ("z_hi", "core")]).astype(jnp.int32)
    carried = contract(place, units, mine, other, n_x, n_zl)
    carried, losses_here = lax.optimization_barrier((carried, losses_here))
    carried = exchange(carried, "y")
    carried = carried.reshape(n_y, part, feat)
    first_grad = jnp.sum(carried.astype(jnp.float32), axis=0).astype(jnp.bfloat16)
    return (attended, losses_here[None, :], first_grad)


def solution(mesh):
    names = ("z_lo", "x", "y", "z_hi", "core")
    fine = Mesh(mesh.devices.reshape(4, 4, 8, 2, 2), names)
    ctx, dp = names[2:], names[:2]
    placed = (
        P(ctx, dp),
        P(ctx, dp),
        P(ctx, dp),
        P(),
        P(dp, None),
        P(),
        P(),
        P(ctx, None, None),
        P(ctx, None),
        P(ctx),
    )
    return jax.shard_map(
        shards,
        mesh=fine,
        in_specs=placed,
        out_specs=(P(ctx, dp), P(ctx, dp), P(ctx, dp)),
        check_vma=False,
    )
```
